32 devices in a mesh: ctx: 8 (over z, x), tp: 4 (over y, core).
Axes of the slice: x: 2, y: 2, z: 4, core: 2. Of those that a mesh axis runs over, the one named last changes fastest.
Arguments:
- projected: bfloat16 [1024, 3, 4096], P('ctx', None, 'tp'), may hold values from -6 to 6
- short_taps: float32 [3, 7, 4096], P(None, None, 'tp'), may hold values from -2 to 2
- residues: float32 [4096, 16], P('tp'), may hold values from -6 to 6
- rates: float32 [4096, 16], P('tp'), may hold values from 0.3 to 64
- skip_gain: float32 [4096], P('tp'), may hold values from -1 to 1
- norm_gain: float32 [4096], P('tp'), may hold values from 0.5 to 1.5
Outputs:
- mixed_out: bfloat16 [1024, 4096], P('ctx', 'tp')
The draws below stay inside these ranges and needn't reach their ends.
All inputs are finite; a program needn't handle non-finite values.
Results may differ from the reference program's by a relative error of at most 0.008.
Values may be sent and summed in bfloat16 or wider, within the bound.
A program may use at most 64 MiB of HBM per device.

```python
import math
import jax
import jax.numpy as jnp
from jax import lax

D = 4096
MODES = 16
TAPS = 7
LENGTH = 1024


def draw_short_taps(key, part):
    base = jax.random.uniform(key, (3, TAPS, D), jnp.float32, -0.5, 0.5)
    chan = jnp.arange(D, dtype=jnp.int32).astype(jnp.float32) / D
    scale = jnp.power(3.0, 0.75 * chan)
    first = jnp.arange(3, dtype=jnp.int32)[:, None, None] == 0
    return jnp.where(first, base * scale[None, None, :], base)


def block_levels(rng, dims, cuts, smallest, largest):
    def one(dim, blocks):
        heights = jax.random.uniform(jax.random.fold_in(jax.random.fold_in(rng, 6), dim), (blocks,), jnp.float32, smallest / len(cuts), largest / len(cuts))
        return jnp.repeat(jnp.exp(heights), dims[dim] // blocks).reshape((-1,) + (1,) * (len(dims) - dim - 1))

    loudness = one(*cuts[0])
    for cut in cuts[1:]:
        loudness = loudness * one(*cut)
    return loudness


def centred(stream_key, shape, scale, bound, shards=(), held_as=jnp.bfloat16):
    factor_of = block_levels(stream_key, shape, shards, -0.22, 0.18) if shards else 1.0
    drawn = jax.random.normal(stream_key, shape, jnp.float32) * scale * factor_of
    return jnp.minimum(jnp.maximum(drawn, -bound), bound).astype(held_as)


def setup_inputs(seed: int = 0) -> dict:
    key_list = jax.random.split(jax.random.key(seed), 7)
    return {
        "projected": centred(key_list[0], (LENGTH, 3, D), 1.0, 6.0, ((0, 8), (2, 4))),
        "short_taps": draw_short_taps(jax.random.fold_in(key_list[6], 71), 0),
        "residues": centred(key_list[2], (D, MODES), 1.0, 6.0, ((0, 4),), jnp.float32),
        "rates": jnp.clip(jnp.exp(math.log(64.0) - 5.362856 * jax.random.uniform(key_list[3], (D, MODES), jnp.float32) ** block_levels(key_list[3], (D, MODES), ((0, 4),), -0.2, 0.2)), 0.3, 64.0),
        "skip_gain": jnp.clip(jax.random.uniform(key_list[4], (D,), jnp.float32, -1.0, 1.0) * block_levels(key_list[4], (D,), ((0, 4),), -0.4, 0.0), -1.0, 1.0),
        "norm_gain": jnp.clip(1.0 + 0.1 * jax.random.normal(key_list[5], (D,), jnp.float32), 0.5, 1.5),
    }


def reference(projected, short_taps, residues, rates, skip_gain, norm_gain):
    block = min(D, 256)
    count = D // block
    positions = jnp.arange(LENGTH, dtype=jnp.int32).astype(jnp.float32)

    def one_block(index):
        first = (index * block).astype(jnp.int32)
        piece = lax.dynamic_slice_in_dim(projected, first, block, 2).astype(jnp.float32)
        taps = lax.dynamic_slice_in_dim(short_taps, first, block, 2)
        res_block = lax.dynamic_slice_in_dim(residues, first, block, 0)
        rate_block = lax.dynamic_slice_in_dim(rates, first, block, 0)
        skip_block = lax.dynamic_slice_in_dim(skip_gain, first, block, 0)
        padded = jnp.pad(piece, ((TAPS - 1, 0), (0, 0), (0, 0)))
        mixed = jnp.zeros_like(piece)
        for offset in range(TAPS):
            mixed = mixed + taps[None, :, offset, :] * padded[TAPS - 1 - offset:TAPS - 1 - offset + LENGTH]
        query = mixed[:, 0]
        keyed = mixed[:, 1]
        valued = mixed[:, 2]
        product = (keyed * valued).astype(jnp.bfloat16)
        product_wide = lax.optimization_barrier(product).astype(jnp.float32)
        kernel = jnp.zeros((LENGTH, block), jnp.float32)
        for mode in range(MODES):
            kernel = kernel + res_block[:, mode][None, :] * jnp.exp(-(positions[:, None] * rate_block[:, mode][None, :]) / LENGTH)
        kernel = kernel / math.sqrt(LENGTH)
        spectrum = jnp.fft.rfft(product_wide, n=2 * LENGTH, axis=0) * jnp.fft.rfft(kernel, n=2 * LENGTH, axis=0)
        convolved = jnp.fft.irfft(spectrum, n=2 * LENGTH, axis=0)[:LENGTH]
        long_part = convolved.astype(jnp.bfloat16)
        long_wide = lax.optimization_barrier(long_part).astype(jnp.float32)
        return query * (long_wide + skip_block[None, :] * product_wide)
    blocks = lax.map(one_block, jnp.arange(count, dtype=jnp.int32))
    gated = jnp.transpose(blocks, (1, 0, 2)).reshape(LENGTH, D)
    mean_square = lax.optimization_barrier(jnp.sum(gated * gated, axis=1, keepdims=True)) / D
    return (gated * norm_gain[None, :] / jnp.sqrt(mean_square + 1e-05)).astype(jnp.bfloat16)
```

```python
import functools
import math

import jax
import jax.numpy as jnp
import ml_dtypes
import numpy as np
from jax import lax
from jax.experimental import pallas as pl
from jax.experimental.pallas import tpu as pltpu
from jax.sharding import PartitionSpec as P

LANES = 128
SUB = 8
HIGHEST = lax.Precision.HIGHEST


def tables(rows):
    freq = (np.arange(rows) + 0.5)[:, None] * (2.0 * math.pi / (2 * rows))
    angle = freq * np.arange(rows)[None, :]
    forward = np.concatenate([np.cos(angle), -np.sin(angle)], 0)
    inverse = forward.T / rows

    def pair(a):
        hi = a.astype(ml_dtypes.bfloat16)
        lo = (a - hi.astype(np.float64)).astype(ml_dtypes.bfloat16)
        return hi, lo

    f_hi, f_lo = pair(forward)
    g_hi, g_lo = pair(inverse)
    return np.concatenate([f_hi, f_lo], 1), g_hi, g_lo


def kernel(
    n, m, modes, taps_n, rows, channels, length,
    proj, taps, res, rates, skip, gain, fwd, inv_hi, inv_lo,
    out,
    x, kv, state, state0, filt, tailw, a8, a128, long, gated, squares,
    send_kv, halo_kv, halo_q, end_f, end_b, ends, sums,
    halo_send, halo_recv, end_send, end_recv, sum_send, sum_recv,
):
    me = lax.axis_index("ctx")
    lane_rank = lax.axis_index("tp")
    tiles = channels // LANES
    blocks = rows // SUB
    dot = functools.partial(jnp.dot, preferred_element_type=jnp.float32)

    barrier = pltpu.get_barrier_semaphore()

    def greet(i, _):
        pl.semaphore_signal(barrier, inc=1, device_id={"ctx": i}, device_id_type=pl.DeviceIdType.MESH)
        return 0

    lax.fori_loop(0, me, greet, 0)
    for d in range(1, m):
        pl.semaphore_signal(
            barrier, inc=1, device_id={"tp": lax.rem(lane_rank + d, m)}, device_id_type=pl.DeviceIdType.MESH
        )

    rim_k = proj[1, rows - 16 :, :].astype(jnp.float32)[SUB:]
    rim_v = proj[2, rows - 16 :, :].astype(jnp.float32)[SUB:]
    send_kv[...] = jnp.concatenate([rim_k, rim_v], 0).astype(jnp.bfloat16)
    pl.semaphore_wait(barrier, n - 1 - me + m - 1)

    def halo_copies():
        right = lax.rem(me + 1, n)
        first = pltpu.make_async_remote_copy(
            src_ref=send_kv, dst_ref=halo_kv, send_sem=halo_send.at[0], recv_sem=halo_recv.at[0],
            device_id={"ctx": right}, device_id_type=pl.DeviceIdType.MESH,
        )
        second = pltpu.make_async_remote_copy(
            src_ref=proj.at[0, pl.ds(rows - 16, 16)], dst_ref=halo_q, send_sem=halo_send.at[1],
            recv_sem=halo_recv.at[1], device_id={"ctx": right}, device_id_type=pl.DeviceIdType.MESH,
        )
        return first, second

    @pl.when(me < n - 1)
    def _():
        first, second = halo_copies()
        first.start()
        second.start()

    sub = lax.broadcasted_iota(jnp.int32, (SUB, LANES), 0).astype(jnp.float32)
    scale = 1.0 / math.sqrt(length)
    rate_all = rates[...]
    a8[...] = jnp.exp(-(rate_all * SUB) / length)
    a128[...] = jnp.exp(-(rate_all * rows) / length)

    def columns(t):
        return pl.ds(pl.multiple_of(t * LANES, LANES), LANES)

    def short(g, t, start, count):
        cols = columns(t)
        total = None
        for j in range(taps_n):
            term = taps[g, j : j + 1, cols] * x[g, t, pl.ds(SUB + start - j, count), :]
            total = term if total is None else total + term
        return total

    def rounded(a):
        return a.astype(jnp.bfloat16).astype(jnp.float32)

    def body_a(t, _):
        cols = columns(t)
        for g in range(3):
            x[g, t, pl.ds(SUB, rows), :] = proj[g, :, cols].astype(jnp.float32)
        kv[t, pl.ds(SUB, rows - SUB), :] = rounded(
            short(1, t, SUB, rows - SUB) * short(2, t, SUB, rows - SUB)
        )
        step = [jnp.broadcast_to(a8[i : i + 1, cols], (SUB, LANES)) for i in range(modes)]
        s = [kv[t, pl.ds(SUB, SUB), :]] * modes
        for b in range(2, blocks):
            u = kv[t, pl.ds(b * SUB, SUB), :]
            s = [step[i] * s[i] + u for i in range(modes)]
        for i in range(modes):
            r = rates[i : i + 1, cols]
            state[i, t] = s[i] * jnp.exp(-(r * (SUB - 1 - sub)) / length)
            state0[i, t] = jnp.exp(-(r * (rows - 1 - sub)) / length)
        return 0

    lax.fori_loop(0, tiles, body_a, 0)

    @pl.when(me > 0)
    def _():
        first, _second = halo_copies()
        first.wait_recv()
        rim = halo_kv[...].astype(jnp.float32)
        for t in range(tiles):
            x[1, t, pl.ds(0, SUB), :] = rim[:SUB, t * LANES : (t + 1) * LANES]
            x[2, t, pl.ds(0, SUB), :] = rim[SUB:, t * LANES : (t + 1) * LANES]

    @pl.when(me == 0)
    def _():
        for g in range(3):
            for t in range(tiles):
                x[g, t, pl.ds(0, SUB), :] = jnp.zeros((SUB, LANES), jnp.float32)

    def body_b(t, _):
        cols = columns(t)
        u = rounded(short(1, t, 0, SUB) * short(2, t, 0, SUB))
        kv[t, pl.ds(0, SUB), :] = u
        for i in range(modes):
            end_f[i : i + 1, cols] = jnp.sum(state[i, t] + state0[i, t] * u, axis=0, keepdims=True)
        return 0

    lax.fori_loop(0, tiles, body_b, 0)
    end_b[...] = end_f[...].astype(jnp.bfloat16)

    def end_copy(slot, target):
        return pltpu.make_async_remote_copy(
            src_ref=end_b, dst_ref=ends.at[slot], send_sem=end_send.at[target], recv_sem=end_recv.at[slot],
            device_id={"ctx": target}, device_id_type=pl.DeviceIdType.MESH,
        )

    def send_end(j, _):
        end_copy(me, j).start()
        return 0

    lax.fori_loop(me + 1, n, send_end, 0)

    def body_c(t, _):
        cols = columns(t)
        step = [jnp.broadcast_to(a8[i : i + 1, cols], (SUB, LANES)) for i in range(modes)]
        w = []
        for i in range(modes):
            r = rates[i : i + 1, cols]
            c = res[i : i + 1, cols] * scale
            w.append(c * jnp.exp(-(r * sub) / length))
            tailw[i, t] = c * jnp.exp(-(r * (sub + 1.0)) / length)
        for b in range(blocks):
            total = w[0]
            for i in range(1, modes):
                total = total + w[i]
            filt[t, pl.ds(b * SUB, SUB), :] = total
            if b < blocks - 1:
                w = [w[i] * step[i] for i in range(modes)]
        return 0

    lax.fori_loop(0, tiles, body_c, 0)

    def body_d(p, _):
        t0 = 2 * p
        u = jnp.concatenate([kv[t0], kv[t0 + 1]], 1).astype(jnp.bfloat16)
        f = jnp.concatenate([filt[t0], filt[t0 + 1]], 1)
        f_hi = f.astype(jnp.bfloat16)
        f_lo = (f - f_hi.astype(jnp.float32)).astype(jnp.bfloat16)
        both = fwd[...]
        us = dot(both, jnp.concatenate([u, u], 0))
        fs = dot(both, jnp.concatenate([f_hi, f_hi], 0)) + dot(both[:, :rows], f_lo)
        ur, ui, fr, fi = us[:rows], us[rows:], fs[:rows], fs[rows:]
        prod = jnp.concatenate([ur * fr - ui * fi, ur * fi + ui * fr], 0)
        p_hi = prod.astype(jnp.bfloat16)
        p_lo = (prod - p_hi.astype(jnp.float32)).astype(jnp.bfloat16)
        y = dot(inv_hi[...], p_hi) + dot(inv_lo[...], p_hi) + dot(inv_hi[...], p_lo)
        long[t0] = y[:, :LANES]
        long[t0 + 1] = y[:, LANES:]
        return 0

    lax.fori_loop(0, tiles // 2, body_d, 0)

    @pl.when(me > 0)
    def _():
        _first, second = halo_copies()
        second.wait_recv()
        rim = halo_q[...].astype(jnp.float32)[SUB:]
        for t in range(tiles):
            x[0, t, pl.ds(0, SUB), :] = rim[:, t * LANES : (t + 1) * LANES]

    def body_q(t, _):
        gated[t] = short(0, t, 0, rows)
        return 0

    lax.fori_loop(0, tiles, body_q, 0)

    def gather(i, carry):
        end_copy(i, i).wait_recv()
        return carry * a128[...] + ends[i].astype(jnp.float32)

    end_f[...] = lax.fori_loop(0, me, gather, jnp.zeros((modes, channels), jnp.float32))
    squares[...] = jnp.zeros_like(squares)

    def body_e(t, _):
        cols = columns(t)
        step = [jnp.broadcast_to(a8[i : i + 1, cols], (SUB, LANES)) for i in range(modes)]
        w = [tailw[i, t] * end_f[i : i + 1, cols] for i in range(modes)]
        direct = skip[:, cols]
        for b in range(blocks):
            here = pl.ds(b * SUB, SUB)
            total = w[0]
            for i in range(1, modes):
                total = total + w[i]
            y = rounded(long[t, here, :] + total)
            g = gated[t, here, :] * (y + direct * kv[t, here, :])
            gated[t, here, :] = g
            squares[here, :] += g * g
            if b < blocks - 1:
                w = [w[i] * step[i] for i in range(modes)]
        return 0

    lax.fori_loop(0, tiles, body_e, 0)

    ones = jnp.ones((SUB, LANES), jnp.float32)
    mine = lax.dot_general(
        ones, squares[...], (((1,), (1,)), ((), ())), precision=HIGHEST, preferred_element_type=jnp.float32
    )
    sums[lane_rank] = mine

    def sum_copy(d, slot):
        return pltpu.make_async_remote_copy(
            src_ref=sums.at[lane_rank], dst_ref=sums.at[slot], send_sem=sum_send.at[d],
            recv_sem=sum_recv.at[slot], device_id={"tp": lax.rem(lane_rank + d, m)},
            device_id_type=pl.DeviceIdType.MESH,
        )

    for d in range(1, m):
        sum_copy(d, lane_rank).start()
    for d in range(1, m):
        sum_copy(d, lax.rem(lane_rank + d, m)).wait_recv()
    total = sums[0]
    for d in range(1, m):
        total = total + sums[d]
    inverse = 1.0 / jnp.sqrt(total / (channels * m) + 1e-05)
    spread = lax.dot_general(
        inverse, ones * (1.0 / SUB), (((0,), (0,)), ((), ())), precision=HIGHEST,
        preferred_element_type=jnp.float32,
    )

    for t in range(tiles):
        cols = slice(t * LANES, (t + 1) * LANES)
        out[:, cols] = (gated[t] * gain[:, cols] * spread).astype(jnp.bfloat16)

    @pl.when(me < n - 1)
    def _():
        first, second = halo_copies()
        first.wait_send()
        second.wait_send()

    def finish(j, _):
        end_copy(me, j).wait_send()
        return 0

    lax.fori_loop(me + 1, n, finish, 0)
    for d in range(1, m):
        sum_copy(d, lane_rank).wait_send()


def solution(mesh):
    n, m = mesh.shape["ctx"], mesh.shape["tp"]

    def shards(projected, short_taps, residues, rates, skip_gain, norm_gain):
        rows, _, channels = projected.shape
        modes = rates.shape[1]
        tiles = channels // LANES
        f32, bf16 = jnp.float32, jnp.bfloat16
        fwd, inv_hi, inv_lo = (jnp.asarray(a) for a in tables(rows))
        tile3 = pltpu.VMEM((tiles, rows, LANES), f32)
        modal = pltpu.VMEM((modes, tiles, SUB, LANES), f32)
        flat = pltpu.VMEM((modes, channels), f32)
        dma = pltpu.SemaphoreType.DMA
        return pl.pallas_call(
            functools.partial(kernel, n, m, modes, short_taps.shape[1], rows, channels, rows * n),
            out_shape=jax.ShapeDtypeStruct((rows, channels), bf16),
            in_specs=[pl.BlockSpec(memory_space=pltpu.VMEM)] * 9,
            out_specs=pl.BlockSpec(memory_space=pltpu.VMEM),
            scratch_shapes=[
                pltpu.VMEM((3, tiles, rows + SUB, LANES), f32),
                tile3, modal, modal, tile3, modal, flat, flat, tile3, tile3,
                pltpu.VMEM((rows, LANES), f32),
                pltpu.VMEM((16, channels), bf16),
                pltpu.VMEM((16, channels), bf16),
                pltpu.VMEM((16, channels), bf16),
                flat,
                pltpu.VMEM((modes, channels), bf16),
                pltpu.VMEM((n, modes, channels), bf16),
                pltpu.VMEM((m, SUB, LANES), f32),
                dma((2,)), dma((2,)), dma((n,)), dma((n,)), dma((m,)), dma((m,)),
            ],
            compiler_params=pltpu.CompilerParams(
                collective_id=0, has_side_effects=True, vmem_limit_bytes=32 * 1024 * 1024
            ),
        )(
            jnp.transpose(projected, (1, 0, 2)), short_taps, residues.T, rates.T,
            skip_gain[None, :], norm_gain[None, :], fwd, inv_hi, inv_lo,
        )

    return jax.shard_map(
        shards,
        mesh=mesh,
        in_specs=(
            P("ctx", None, "tp"),
            P(None, None, "tp"),
            P("tp", None),
            P("tp", None),
            P("tp"),
            P("tp"),
        ),
        out_specs=P("ctx", "tp"),
        check_vma=False,
    )
```

```python
import functools
import math

import jax
import jax.numpy as jnp
import ml_dtypes
import numpy as np
from jax import lax
from jax.experimental import pallas as pl
from jax.experimental.pallas import tpu as pltpu
from jax.sharding import PartitionSpec as P

LANES = 128
SUB = 8
HIGHEST = lax.Precision.HIGHEST


def tables(rows):
    freq = (np.arange(rows) + 0.5)[:, None] * (2.0 * math.pi / (2 * rows))
    angle = freq * np.arange(rows)[None, :]
    forward = np.concatenate([np.cos(angle), -np.sin(angle)], 0)
    inverse = forward.T / rows

    def pair(a):
        hi = a.astype(ml_dtypes.bfloat16)
        lo = (a - hi.astype(np.float64)).astype(ml_dtypes.bfloat16)
        return hi, lo

    f_hi, f_lo = pair(forward)
    g_hi, g_lo = pair(inverse)
    return np.concatenate([f_hi, f_lo], 1), g_hi, g_lo


def kernel(
    n, m, modes, taps_n, rows, channels, length,
    proj_h, taps_h, res_h, rates_h, skip_h, gain_h, fwd_h, inv_hi_h, inv_lo_h,
    out,
    rim, proj, taps, res, rates, skip, gain, fwd, inv_hi, inv_lo, load_sem,
    x, kv, state, state0, filt, tailw, a8, a128, long, gated, squares,
    send_kv, halo_kv, halo_q, end_f, end_b, ends, sums,
    halo_send, halo_recv, end_send, end_recv, sum_send, sum_recv,
):
    me = lax.axis_index("ctx")
    lane_rank = lax.axis_index("tp")
    tiles = channels // LANES
    blocks = rows // SUB
    dot = functools.partial(jnp.dot, preferred_element_type=jnp.float32)

    pairs = [
        (proj_h.at[pl.ds(1, 2), pl.ds(rows - 16, 16)], rim),
        (proj_h.at[pl.ds(1, 2)], proj.at[pl.ds(1, 2)]),
        (taps_h, taps), (rates_h, rates), (res_h, res),
        (proj_h.at[0], proj.at[0]),
        (fwd_h, fwd), (inv_hi_h, inv_hi), (inv_lo_h, inv_lo), (skip_h, skip), (gain_h, gain),
    ]
    loads = [pltpu.make_async_copy(a, b, load_sem.at[i]) for i, (a, b) in enumerate(pairs)]
    for load in loads:
        load.start()

    barrier = pltpu.get_barrier_semaphore()

    def greet(i, _):
        pl.semaphore_signal(barrier, inc=1, device_id={"ctx": i}, device_id_type=pl.DeviceIdType.MESH)
        return 0

    lax.fori_loop(0, me, greet, 0)
    for d in range(1, m):
        pl.semaphore_signal(
            barrier, inc=1, device_id={"tp": lax.rem(lane_rank + d, m)}, device_id_type=pl.DeviceIdType.MESH
        )

    loads[0].wait()
    rim_k = rim[0].astype(jnp.float32)[SUB:]
    rim_v = rim[1].astype(jnp.float32)[SUB:]
    send_kv[...] = jnp.concatenate([rim_k, rim_v], 0).astype(jnp.bfloat16)
    pl.semaphore_wait(barrier, n - 1 - me + m - 1)

    def halo_copies():
        right = lax.rem(me + 1, n)
        first = pltpu.make_async_remote_copy(
            src_ref=send_kv, dst_ref=halo_kv, send_sem=halo_send.at[0], recv_sem=halo_recv.at[0],
            device_id={"ctx": right}, device_id_type=pl.DeviceIdType.MESH,
        )
        second = pltpu.make_async_remote_copy(
            src_ref=proj_h.at[0, pl.ds(rows - 16, 16)], dst_ref=halo_q, send_sem=halo_send.at[1],
            recv_sem=halo_recv.at[1], device_id={"ctx": right}, device_id_type=pl.DeviceIdType.MESH,
        )
        return first, second

    @pl.when(me < n - 1)
    def _():
        first, second = halo_copies()
        first.start()
        second.start()

    sub = lax.broadcasted_iota(jnp.int32, (SUB, LANES), 0).astype(jnp.float32)
    scale = 1.0 / math.sqrt(length)
    for i in (1, 2, 3):
        loads[i].wait()
    rate_all = rates[...]
    a8[...] = jnp.exp(-(rate_all * SUB) / length)
    a128[...] = jnp.exp(-(rate_all * rows) / length)

    def columns(t):
        return pl.ds(pl.multiple_of(t * LANES, LANES), LANES)

    def short(g, t, start, count):
        cols = columns(t)
        total = None
        for j in range(taps_n):
            term = taps[g, j : j + 1, cols] * x[g, t, pl.ds(SUB + start - j, count), :]
            total = term if total is None else total + term
        return total

    def rounded(a):
        return a.astype(jnp.bfloat16).astype(jnp.float32)

    def body_a(t, _):
        cols = columns(t)
        for g in (1, 2):
            x[g, t, pl.ds(SUB, rows), :] = proj[g, :, cols].astype(jnp.float32)
        kv[t, pl.ds(SUB, rows - SUB), :] = rounded(
            short(1, t, SUB, rows - SUB) * short(2, t, SUB, rows - SUB)
        )
        step = [jnp.broadcast_to(a8[i : i + 1, cols], (SUB, LANES)) for i in range(modes)]
        s = [kv[t, pl.ds(SUB, SUB), :]] * modes
        for b in range(2, blocks):
            u = kv[t, pl.ds(b * SUB, SUB), :]
            s = [step[i] * s[i] + u for i in range(modes)]
        for i in range(modes):
            r = rates[i : i + 1, cols]
            state[i, t] = s[i] * jnp.exp(-(r * (SUB - 1 - sub)) / length)
            state0[i, t] = jnp.exp(-(r * (rows - 1 - sub)) / length)
        return 0

    lax.fori_loop(0, tiles, body_a, 0)

    @pl.when(me > 0)
    def _():
        first, _second = halo_copies()
        first.wait_recv()
        tail = halo_kv[...].astype(jnp.float32)
        for t in range(tiles):
            x[1, t, pl.ds(0, SUB), :] = tail[:SUB, t * LANES : (t + 1) * LANES]
            x[2, t, pl.ds(0, SUB), :] = tail[SUB:, t * LANES : (t + 1) * LANES]

    @pl.when(me == 0)
    def _():
        for g in range(3):
            for t in range(tiles):
                x[g, t, pl.ds(0, SUB), :] = jnp.zeros((SUB, LANES), jnp.float32)

    def body_b(t, _):
        cols = columns(t)
        u = rounded(short(1, t, 0, SUB) * short(2, t, 0, SUB))
        kv[t, pl.ds(0, SUB), :] = u
        for i in range(modes):
            end_f[i : i + 1, cols] = jnp.sum(state[i, t] + state0[i, t] * u, axis=0, keepdims=True)
        return 0

    lax.fori_loop(0, tiles, body_b, 0)
    end_b[...] = end_f[...].astype(jnp.bfloat16)

    def end_copy(slot, target):
        return pltpu.make_async_remote_copy(
            src_ref=end_b, dst_ref=ends.at[slot], send_sem=end_send.at[target], recv_sem=end_recv.at[slot],
            device_id={"ctx": target}, device_id_type=pl.DeviceIdType.MESH,
        )

    def send_end(j, _):
        end_copy(me, j).start()
        return 0

    lax.fori_loop(me + 1, n, send_end, 0)

    loads[4].wait()

    def body_c(t, _):
        cols = columns(t)
        step = [jnp.broadcast_to(a8[i : i + 1, cols], (SUB, LANES)) for i in range(modes)]
        w = []
        for i in range(modes):
            r = rates[i : i + 1, cols]
            c = res[i : i + 1, cols] * scale
            w.append(c * jnp.exp(-(r * sub) / length))
            tailw[i, t] = c * jnp.exp(-(r * (sub + 1.0)) / length)
        for b in range(blocks):
            total = w[0]
            for i in range(1, modes):
                total = total + w[i]
            filt[t, pl.ds(b * SUB, SUB), :] = total
            if b < blocks - 1:
                w = [w[i] * step[i] for i in range(modes)]
        return 0

    lax.fori_loop(0, tiles, body_c, 0)

    for i in range(5, len(loads)):
        loads[i].wait()

    def body_d(p, _):
        t0 = 2 * p
        u = jnp.concatenate([kv[t0], kv[t0 + 1]], 1).astype(jnp.bfloat16)
        f = jnp.concatenate([filt[t0], filt[t0 + 1]], 1)
        f_hi = f.astype(jnp.bfloat16)
        f_lo = (f - f_hi.astype(jnp.float32)).astype(jnp.bfloat16)
        both = fwd[...]
        us = dot(both, jnp.concatenate([u, u], 0))
        fs = dot(both, jnp.concatenate([f_hi, f_hi], 0)) + dot(both[:, :rows], f_lo)
        ur, ui, fr, fi = us[:rows], us[rows:], fs[:rows], fs[rows:]
        prod = jnp.concatenate([ur * fr - ui * fi, ur * fi + ui * fr], 0)
        p_hi = prod.astype(jnp.bfloat16)
        p_lo = (prod - p_hi.astype(jnp.float32)).astype(jnp.bfloat16)
        y = dot(inv_hi[...], p_hi) + dot(inv_lo[...], p_hi) + dot(inv_hi[...], p_lo)
        long[t0] = y[:, :LANES]
        long[t0 + 1] = y[:, LANES:]
        return 0

    lax.fori_loop(0, tiles // 2, body_d, 0)

    @pl.when(me > 0)
    def _():
        _first, second = halo_copies()
        second.wait_recv()
        tail = halo_q[...].astype(jnp.float32)[SUB:]
        for t in range(tiles):
            x[0, t, pl.ds(0, SUB), :] = tail[:, t * LANES : (t + 1) * LANES]

    def body_q(t, _):
        x[0, t, pl.ds(SUB, rows), :] = proj[0, :, columns(t)].astype(jnp.float32)
        gated[t] = short(0, t, 0, rows)
        return 0

    lax.fori_loop(0, tiles, body_q, 0)

    def gather(i, carry):
        end_copy(i, i).wait_recv()
        return carry * a128[...] + ends[i].astype(jnp.float32)

    end_f[...] = lax.fori_loop(0, me, gather, jnp.zeros((modes, channels), jnp.float32))
    squares[...] = jnp.zeros_like(squares)

    def body_e(t, _):
        cols = columns(t)
        step = [jnp.broadcast_to(a8[i : i + 1, cols], (SUB, LANES)) for i in range(modes)]
        w = [tailw[i, t] * end_f[i : i + 1, cols] for i in range(modes)]
        direct = skip[:, cols]
        for b in range(blocks):
            here = pl.ds(b * SUB, SUB)
            total = w[0]
            for i in range(1, modes):
                total = total + w[i]
            y = rounded(long[t, here, :] + total)
            g = gated[t, here, :] * (y + direct * kv[t, here, :])
            gated[t, here, :] = g
            squares[here, :] += g * g
            if b < blocks - 1:
                w = [w[i] * step[i] for i in range(modes)]
        return 0

    lax.fori_loop(0, tiles, body_e, 0)

    ones = jnp.ones((SUB, LANES), jnp.float32)
    mine = lax.dot_general(
        ones, squares[...], (((1,), (1,)), ((), ())), precision=HIGHEST, preferred_element_type=jnp.float32
    )
    sums[lane_rank] = mine

    def sum_copy(d, slot):
        return pltpu.make_async_remote_copy(
            src_ref=sums.at[lane_rank], dst_ref=sums.at[slot], send_sem=sum_send.at[d],
            recv_sem=sum_recv.at[slot], device_id={"tp": lax.rem(lane_rank + d, m)},
            device_id_type=pl.DeviceIdType.MESH,
        )

    for d in range(1, m):
        sum_copy(d, lane_rank).start()
    for d in range(1, m):
        sum_copy(d, lax.rem(lane_rank + d, m)).wait_recv()
    total = sums[0]
    for d in range(1, m):
        total = total + sums[d]
    inverse = 1.0 / jnp.sqrt(total / (channels * m) + 1e-05)
    spread = lax.dot_general(
        inverse, ones * (1.0 / SUB), (((0,), (0,)), ((), ())), precision=HIGHEST,
        preferred_element_type=jnp.float32,
    )

    for t in range(tiles):
        cols = slice(t * LANES, (t + 1) * LANES)
        out[:, cols] = (gated[t] * gain[:, cols] * spread).astype(jnp.bfloat16)

    @pl.when(me < n - 1)
    def _():
        first, second = halo_copies()
        first.wait_send()
        second.wait_send()

    def finish(j, _):
        end_copy(me, j).wait_send()
        return 0

    lax.fori_loop(me + 1, n, finish, 0)
    for d in range(1, m):
        sum_copy(d, lane_rank).wait_send()


def solution(mesh):
    n, m = mesh.shape["ctx"], mesh.shape["tp"]

    def shards(projected, short_taps, residues, rates, skip_gain, norm_gain):
        rows, _, channels = projected.shape
        modes = rates.shape[1]
        tiles = channels // LANES
        f32, bf16 = jnp.float32, jnp.bfloat16
        fwd, inv_hi, inv_lo = (jnp.asarray(a) for a in tables(rows))
        tile3 = pltpu.VMEM((tiles, rows, LANES), f32)
        modal = pltpu.VMEM((modes, tiles, SUB, LANES), f32)
        flat = pltpu.VMEM((modes, channels), f32)
        dma = pltpu.SemaphoreType.DMA
        return pl.pallas_call(
            functools.partial(kernel, n, m, modes, short_taps.shape[1], rows, channels, rows * n),
            out_shape=jax.ShapeDtypeStruct((rows, channels), bf16),
            in_specs=[pl.BlockSpec(memory_space=pltpu.HBM)] * 9,
            out_specs=pl.BlockSpec(memory_space=pltpu.VMEM),
            scratch_shapes=[
                pltpu.VMEM((2, 16, channels), bf16),
                pltpu.VMEM(projected.shape[1:2] + (rows, channels), bf16),
                pltpu.VMEM(short_taps.shape, f32), flat, flat,
                pltpu.VMEM((1, channels), f32), pltpu.VMEM((1, channels), f32),
                pltpu.VMEM(fwd.shape, bf16), pltpu.VMEM(inv_hi.shape, bf16), pltpu.VMEM(inv_lo.shape, bf16),
                dma((11,)),
                pltpu.VMEM((3, tiles, rows + SUB, LANES), f32),
                tile3, modal, modal, tile3, modal, flat, flat, tile3, tile3,
                pltpu.VMEM((rows, LANES), f32),
                pltpu.VMEM((16, channels), bf16),
                pltpu.VMEM((16, channels), bf16),
                pltpu.VMEM((16, channels), bf16),
                flat,
                pltpu.VMEM((modes, channels), bf16),
                pltpu.VMEM((n, modes, channels), bf16),
                pltpu.VMEM((m, SUB, LANES), f32),
                dma((2,)), dma((2,)), dma((n,)), dma((n,)), dma((m,)), dma((m,)),
            ],
            compiler_params=pltpu.CompilerParams(
                collective_id=0, has_side_effects=True, vmem_limit_bytes=60 * 1024 * 1024
            ),
        )(
            jnp.transpose(projected, (1, 0, 2)), short_taps, residues.T, rates.T,
            skip_gain[None, :], norm_gain[None, :], fwd, inv_hi, inv_lo,
        )

    return jax.shard_map(
        shards,
        mesh=mesh,
        in_specs=(
            P("ctx", None, "tp"),
            P(None, None, "tp"),
            P("tp", None),
            P("tp", None),
            P("tp"),
            P("tp"),
        ),
        out_specs=P("ctx", "tp"),
        check_vma=False,
    )
```

```python
import functools
import math

import jax
import jax.numpy as jnp
import ml_dtypes
import numpy as np
from jax import lax
from jax.experimental import pallas as pl
from jax.experimental.pallas import tpu as pltpu
from jax.sharding import PartitionSpec as P

LANES = 128
SUB = 8


def tables(rows):
    freq = (np.arange(rows) + 0.5)[:, None] * (2.0 * math.pi / (2 * rows))
    angle = freq * np.arange(rows)[None, :]
    forward = np.concatenate([np.cos(angle), -np.sin(angle)], 0)
    inverse = forward.T / rows

    def pair(a):
        hi = a.astype(ml_dtypes.bfloat16)
        lo = (a - hi.astype(np.float64)).astype(ml_dtypes.bfloat16)
        return hi, lo

    f_hi, f_lo = pair(forward)
    g_hi, g_lo = pair(inverse)
    return np.concatenate([f_hi, f_lo, f_hi], 1), np.concatenate([g_hi, g_lo], 0)


def kernel(
    n, m, modes, taps_n, rows, channels, length,
    proj_h, taps_h, res_h, rates_h, skip_h, gain_h, fwd_h, inv_h,
    out,
    rim, proj, taps, res, rates, skip, gain, fwd, inv, load_sem,
    x, kv, state, state0, filt, spec_f, spec_u, prod_hi, prod_lo, tailw, a8, a128, long, gated, squares,
    send_kv, halo_kv, halo_q, end_f, end_b, mate_b, pair_b, ends, sums,
    halo_send, halo_recv, end_send, end_recv, sum_send, sum_recv, mate_sem,
):
    me = lax.axis_index("ctx")
    lane_rank = lax.axis_index("tp")
    tiles = channels // LANES
    blocks = rows // SUB
    dot = functools.partial(jnp.dot, preferred_element_type=jnp.float32)

    pairs = [
        (proj_h.at[pl.ds(1, 2), pl.ds(rows - 16, 16)], rim),
        (proj_h.at[pl.ds(1, 2)], proj.at[pl.ds(1, 2)]),
        (taps_h, taps), (rates_h, rates), (res_h, res),
        (proj_h.at[0], proj.at[0]),
        (fwd_h, fwd), (inv_h, inv), (skip_h, skip), (gain_h, gain),
    ]
    loads = [pltpu.make_async_copy(a, b, load_sem.at[i]) for i, (a, b) in enumerate(pairs)]
    for load in loads:
        load.start()

    barrier = pltpu.get_barrier_semaphore()

    def greet(target):
        pl.semaphore_signal(barrier, inc=1, device_id={"ctx": target}, device_id_type=pl.DeviceIdType.MESH)

    pair, side = lax.div(me, 2), lax.rem(me, 2)

    @pl.when(me > 0)
    def _():
        greet(me - 1)

    greet(me + 1 - 2 * side)

    def greet_like(i, _):
        greet(2 * i + side)
        return 0

    lax.fori_loop(0, pair, greet_like, 0)
    for d in range(1, m):
        pl.semaphore_signal(
            barrier, inc=1, device_id={"tp": lax.rem(lane_rank + d, m)}, device_id_type=pl.DeviceIdType.MESH
        )

    loads[0].wait()
    rim_k = rim[0].astype(jnp.float32)[SUB:]
    rim_v = rim[1].astype(jnp.float32)[SUB:]
    send_kv[...] = jnp.concatenate([rim_k, rim_v], 0).astype(jnp.bfloat16)
    pl.semaphore_wait(barrier, jnp.where(me < n - 1, 1, 0) + 1 + (n // 2 - 1 - pair) + m - 1)

    def halo_copies():
        right = lax.rem(me + 1, n)
        first = pltpu.make_async_remote_copy(
            src_ref=send_kv, dst_ref=halo_kv, send_sem=halo_send.at[0], recv_sem=halo_recv.at[0],
            device_id={"ctx": right}, device_id_type=pl.DeviceIdType.MESH,
        )
        second = pltpu.make_async_remote_copy(
            src_ref=proj_h.at[0, pl.ds(rows - 16, 16)], dst_ref=halo_q, send_sem=halo_send.at[1],
            recv_sem=halo_recv.at[1], device_id={"ctx": right}, device_id_type=pl.DeviceIdType.MESH,
        )
        return first, second

    @pl.when(me < n - 1)
    def _():
        first, second = halo_copies()
        first.start()
        second.start()

    sub = lax.broadcasted_iota(jnp.int32, (SUB, LANES), 0).astype(jnp.float32)
    scale = 1.0 / math.sqrt(length)
    for i in (1, 2, 3):
        loads[i].wait()
    rate_all = rates[...]
    a8[...] = jnp.exp(-(rate_all * SUB) / length)
    a128[...] = jnp.exp(-(rate_all * rows) / length)

    def columns(t):
        return pl.ds(pl.multiple_of(t * LANES, LANES), LANES)

    def short(g, t, start, count):
        cols = slice(t * LANES, (t + 1) * LANES) if isinstance(t, int) else columns(t)
        total = None
        for j in range(taps_n):
            term = taps[g, j : j + 1, cols] * x[g, t, pl.ds(SUB + start - j, count), :]
            total = term if total is None else total + term
        return total

    def tree(terms):
        while len(terms) > 1:
            terms = [a + b for a, b in zip(terms[::2], terms[1::2])] + terms[len(terms) // 2 * 2 :]
        return terms[0]

    def rounded(a):
        return a.astype(jnp.bfloat16).astype(jnp.float32)

    def body_a(t, _):
        cols = columns(t)
        for g in (1, 2):
            x[g, t, pl.ds(SUB, rows), :] = proj[g, :, cols].astype(jnp.float32)
        kv[t, pl.ds(SUB, rows - SUB), :] = rounded(
            short(1, t, SUB, rows - SUB) * short(2, t, SUB, rows - SUB)
        )
        step = [jnp.broadcast_to(a8[i : i + 1, cols], (SUB, LANES)) for i in range(modes)]
        s = [kv[t, pl.ds(SUB, SUB), :]] * modes
        for b in range(2, blocks):
            u = kv[t, pl.ds(b * SUB, SUB), :]
            s = [step[i] * s[i] + u for i in range(modes)]
        for i in range(modes):
            r = rates[i : i + 1, cols]
            state[i, t] = s[i] * jnp.exp(-(r * (SUB - 1 - sub)) / length)
            state0[i, t] = jnp.exp(-(r * (rows - 1 - sub)) / length)
        return 0

    lax.fori_loop(0, tiles, body_a, 0)

    @pl.when(me > 0)
    def _():
        first, _second = halo_copies()
        first.wait_recv()
        tail = halo_kv[...].astype(jnp.float32)
        for t in range(tiles):
            x[1, t, pl.ds(0, SUB), :] = tail[:SUB, t * LANES : (t + 1) * LANES]
            x[2, t, pl.ds(0, SUB), :] = tail[SUB:, t * LANES : (t + 1) * LANES]

    @pl.when(me == 0)
    def _():
        for g in range(3):
            for t in range(tiles):
                x[g, t, pl.ds(0, SUB), :] = jnp.zeros((SUB, LANES), jnp.float32)

    for t in range(tiles):
        cols = slice(t * LANES, (t + 1) * LANES)
        u = rounded(short(1, t, 0, SUB) * short(2, t, 0, SUB))
        kv[t, pl.ds(0, SUB), :] = u
        for i in range(modes):
            end_f[i : i + 1, cols] = jnp.sum(state[i, t] + state0[i, t] * u, axis=0, keepdims=True)
    end_b[...] = end_f[...].astype(jnp.bfloat16)

    mate = me + 1 - 2 * lax.rem(me, 2)
    pairs_n = n // 2

    mate_copy = pltpu.make_async_remote_copy(
        src_ref=end_b, dst_ref=mate_b, send_sem=mate_sem.at[0], recv_sem=mate_sem.at[1],
        device_id={"ctx": mate}, device_id_type=pl.DeviceIdType.MESH,
    )
    mate_copy.start()

    def end_copy(slot, target):
        return pltpu.make_async_remote_copy(
            src_ref=pair_b, dst_ref=ends.at[slot], send_sem=end_send.at[target], recv_sem=end_recv.at[slot],
            device_id={"ctx": 2 * target + side}, device_id_type=pl.DeviceIdType.MESH,
        )

    def send_end(j, _):
        end_copy(pair, j).start()
        return 0

    loads[4].wait()

    def body_c(t, _):
        cols = columns(t)
        step = [jnp.broadcast_to(a8[i : i + 1, cols], (SUB, LANES)) for i in range(modes)]
        w = []
        for i in range(modes):
            r = rates[i : i + 1, cols]
            c = res[i : i + 1, cols] * scale
            w.append(c * jnp.exp(-(r * sub) / length))
            tailw[i, t] = c * jnp.exp(-(r * (sub + 1.0)) / length)
        for b in range(0, blocks, 2):
            first = tree(w)
            w = [w[i] * step[i] for i in range(modes)]
            both = jnp.concatenate([first, tree(w)], 0)
            if b < blocks - 2:
                w = [w[i] * step[i] for i in range(modes)]
            hi = both.astype(jnp.bfloat16)
            lo = (both - hi.astype(jnp.float32)).astype(jnp.bfloat16)
            filt[pl.ds(b * SUB, 2 * SUB), cols] = hi
            filt[pl.ds(rows + b * SUB, 2 * SUB), cols] = hi
            filt[pl.ds(2 * rows + b * SUB, 2 * SUB), cols] = lo
        return 0

    lax.fori_loop(0, tiles, body_c, 0)

    for i in range(5, len(loads)):
        loads[i].wait()

    mate_copy.wait_recv()
    other = mate_b[...].astype(jnp.float32)
    early = jnp.where(side == 0, end_f[...], other)
    late = jnp.where(side == 0, other, end_f[...])
    pair_b[...] = (early * a128[...] + late).astype(jnp.bfloat16)
    lax.fori_loop(pair + 1, pairs_n, send_end, 0)

    width = 2 * LANES
    groups = [slice(c, c + width) for c in range(0, channels, width)]
    for c in groups:
        t0 = c.start // LANES
        u = jnp.concatenate([kv[t0], kv[t0 + 1]], 1).astype(jnp.bfloat16)
        spec_f[:, c] = dot(fwd[...], filt[:, c])
        spec_u[:, c] = dot(fwd[:, : 2 * rows], jnp.concatenate([u, u], 0))
    for c in groups:
        ur, ui, fr, fi = spec_u[:rows, c], spec_u[rows:, c], spec_f[:rows, c], spec_f[rows:, c]
        for at, part in ((0, ur * fr - ui * fi), (rows, ur * fi + ui * fr)):
            hi = part.astype(jnp.bfloat16)
            prod_hi[at : at + rows, c] = hi
            prod_lo[at : at + rows, c] = (part - hi.astype(jnp.float32)).astype(jnp.bfloat16)
    for c in groups:
        t0 = c.start // LANES
        y = dot(inv[...], prod_hi[:, c])
        y = y[:rows] + y[rows:] + dot(inv[:rows], prod_lo[:, c])
        long[t0] = y[:, :LANES]
        long[t0 + 1] = y[:, LANES:]

    @pl.when(me > 0)
    def _():
        _first, second = halo_copies()
        second.wait_recv()
        tail = halo_q[...].astype(jnp.float32)[SUB:]
        for t in range(tiles):
            x[0, t, pl.ds(0, SUB), :] = tail[:, t * LANES : (t + 1) * LANES]

    def body_q(t, _):
        x[0, t, pl.ds(SUB, rows), :] = proj[0, :, columns(t)].astype(jnp.float32)
        gated[t] = short(0, t, 0, rows)
        return 0

    lax.fori_loop(0, tiles, body_q, 0)

    def gather(i, carry):
        end_copy(i, i).wait_recv()
        return carry * (a128[...] * a128[...]) + ends[i].astype(jnp.float32)

    carry = lax.fori_loop(0, pair, gather, jnp.zeros((modes, channels), jnp.float32))
    end_f[...] = jnp.where(side == 0, carry, carry * a128[...] + mate_b[...].astype(jnp.float32))
    squares[...] = jnp.zeros_like(squares)

    def body_e(t, _):
        cols = columns(t)
        step = [jnp.broadcast_to(a8[i : i + 1, cols], (SUB, LANES)) for i in range(modes)]
        w = [tailw[i, t] * end_f[i : i + 1, cols] for i in range(modes)]
        direct = skip[:, cols]
        for b in range(blocks):
            here = pl.ds(b * SUB, SUB)
            y = rounded(long[t, here, :] + tree(w))
            g = gated[t, here, :] * (y + direct * kv[t, here, :])
            gated[t, here, :] = g
            squares[here, :] += g * g
            if b < blocks - 1:
                w = [w[i] * step[i] for i in range(modes)]
        return 0

    lax.fori_loop(0, tiles, body_e, 0)

    def halves(a, axis):
        hi = a.astype(jnp.bfloat16)
        return jnp.concatenate([hi, (a - hi.astype(jnp.float32)).astype(jnp.bfloat16)], axis)

    mine = lax.dot_general(
        jnp.ones((2 * SUB, 2 * LANES), jnp.bfloat16), halves(squares[...], 1), (((1,), (1,)), ((), ())),
        preferred_element_type=jnp.float32,
    )[:SUB]
    sums[lane_rank] = mine

    def sum_copy(d, slot):
        return pltpu.make_async_remote_copy(
            src_ref=sums.at[lane_rank], dst_ref=sums.at[slot], send_sem=sum_send.at[d],
            recv_sem=sum_recv.at[slot], device_id={"tp": lax.rem(lane_rank + d, m)},
            device_id_type=pl.DeviceIdType.MESH,
        )

    for d in range(1, m):
        sum_copy(d, lane_rank).start()
    for d in range(1, m):
        sum_copy(d, lax.rem(lane_rank + d, m)).wait_recv()
    total = sums[0]
    for d in range(1, m):
        total = total + sums[d]
    inverse = 1.0 / jnp.sqrt(total / (channels * m) + 1e-05)
    spread = lax.dot_general(
        halves(inverse, 0), jnp.full((2 * SUB, LANES), 1.0 / SUB, jnp.bfloat16), (((0,), (0,)), ((), ())),
        preferred_element_type=jnp.float32,
    )

    for t in range(tiles):
        cols = slice(t * LANES, (t + 1) * LANES)
        out[:, cols] = (gated[t] * gain[:, cols] * spread).astype(jnp.bfloat16)

    @pl.when(me < n - 1)
    def _():
        first, second = halo_copies()
        first.wait_send()
        second.wait_send()

    def finish(j, _):
        end_copy(pair, j).wait_send()
        return 0

    lax.fori_loop(pair + 1, pairs_n, finish, 0)
    mate_copy.wait_send()
    for d in range(1, m):
        sum_copy(d, lane_rank).wait_send()


def solution(mesh):
    n, m = mesh.shape["ctx"], mesh.shape["tp"]

    def shards(projected, short_taps, residues, rates, skip_gain, norm_gain):
        rows, _, channels = projected.shape
        modes = rates.shape[1]
        tiles = channels // LANES
        f32, bf16 = jnp.float32, jnp.bfloat16
        fwd, inv = (jnp.asarray(a) for a in tables(rows))
        tile3 = pltpu.VMEM((tiles, rows, LANES), f32)
        modal = pltpu.VMEM((modes, tiles, SUB, LANES), f32)
        flat = pltpu.VMEM((modes, channels), f32)
        dma = pltpu.SemaphoreType.DMA
        return pl.pallas_call(
            functools.partial(kernel, n, m, modes, short_taps.shape[1], rows, channels, rows * n),
            out_shape=jax.ShapeDtypeStruct((rows, channels), bf16),
            in_specs=[pl.BlockSpec(memory_space=pltpu.HBM)] * 8,
            out_specs=pl.BlockSpec(memory_space=pltpu.VMEM),
            scratch_shapes=[
                pltpu.VMEM((2, 16, channels), bf16),
                pltpu.VMEM(projected.shape[1:2] + (rows, channels), bf16),
                pltpu.VMEM(short_taps.shape, f32), flat, flat,
                pltpu.VMEM((1, channels), f32), pltpu.VMEM((1, channels), f32),
                pltpu.VMEM(fwd.shape, bf16), pltpu.VMEM(inv.shape, bf16),
                dma((10,)),
                pltpu.VMEM((3, tiles, rows + SUB, LANES), f32),
                tile3, modal, modal,
                pltpu.VMEM((3 * rows, channels), bf16),
                pltpu.VMEM((2 * rows, channels), f32), pltpu.VMEM((2 * rows, channels), f32),
                pltpu.VMEM((2 * rows, channels), bf16), pltpu.VMEM((2 * rows, channels), bf16),
                modal, flat, flat, tile3, tile3,
                pltpu.VMEM((rows, LANES), f32),
                pltpu.VMEM((16, channels), bf16),
                pltpu.VMEM((16, channels), bf16),
                pltpu.VMEM((16, channels), bf16),
                flat,
                pltpu.VMEM((modes, channels), bf16),
                pltpu.VMEM((modes, channels), bf16),
                pltpu.VMEM((modes, channels), bf16),
                pltpu.VMEM((n // 2, modes, channels), bf16),
                pltpu.VMEM((m, SUB, LANES), f32),
                dma((2,)), dma((2,)), dma((n // 2,)), dma((n // 2,)), dma((m,)), dma((m,)), dma((2,)),
            ],
            compiler_params=pltpu.CompilerParams(
                collective_id=0, has_side_effects=True, vmem_limit_bytes=60 * 1024 * 1024
            ),
        )(
            jnp.transpose(projected, (1, 0, 2)), short_taps, residues.T, rates.T,
            skip_gain[None, :], norm_gain[None, :], fwd, inv,
        )

    return jax.shard_map(
        shards,
        mesh=mesh,
        in_specs=(
            P("ctx", None, "tp"),
            P(None, None, "tp"),
            P("tp", None),
            P("tp", None),
            P("tp"),
            P("tp"),
        ),
        out_specs=P("ctx", "tp"),
        check_vma=False,
    )
```

```python
import functools
import math

import jax
import jax.numpy as jnp
import ml_dtypes
import numpy as np
from jax import lax
from jax.experimental import pallas as pl
from jax.experimental.pallas import tpu as pltpu
from jax.sharding import PartitionSpec as P

LANES = 128
SUB = 8


def tables(rows):
    freq = (np.arange(rows) + 0.5)[:, None] * (2.0 * math.pi / (2 * rows))
    angle = freq * np.arange(rows)[None, :]
    forward = np.concatenate([np.cos(angle), -np.sin(angle)], 0)
    inverse = forward.T / rows

    def pair(a):
        hi = a.astype(ml_dtypes.bfloat16)
        lo = (a - hi.astype(np.float64)).astype(ml_dtypes.bfloat16)
        return hi, lo

    f_hi, f_lo = pair(forward)
    g_hi, g_lo = pair(inverse)
    return np.concatenate([f_hi, f_lo, f_hi], 1), np.concatenate([g_hi, g_lo], 0)


def kernel(
    n, m, modes, taps_n, rows, channels, length,
    proj_h, taps_h, res_h, rates_h, skip_h, gain_h, fwd_h, inv_h,
    out,
    rim, proj, taps, res, rates, skip, gain, fwd, inv, load_sem,
    a1, a120, x, kv, state, state0, filt, spec_f, spec_u, prod_hi, prod_lo, tailw, a8, a128, long, gated, squares,
    send_kv, halo_kv, halo_q, end_f, end_b, mate_b, pair_b, ends, sums,
    halo_send, halo_recv, end_send, end_recv, sum_send, sum_recv, mate_sem,
):
    me = lax.axis_index("ctx")
    lane_rank = lax.axis_index("tp")
    tiles = channels // LANES
    blocks = rows // SUB
    dot = functools.partial(jnp.dot, preferred_element_type=jnp.float32)

    pairs = [
        (proj_h.at[pl.ds(1, 2), pl.ds(rows - 16, 16)], rim),
        (rates_h, rates), (res_h, res), (taps_h, taps),
        (proj_h.at[pl.ds(1, 2)], proj.at[pl.ds(1, 2)]),
        (proj_h.at[0], proj.at[0]),
        (fwd_h, fwd), (inv_h, inv), (skip_h, skip), (gain_h, gain),
    ]
    loads = [pltpu.make_async_copy(a, b, load_sem.at[i]) for i, (a, b) in enumerate(pairs)]
    for load in loads:
        load.start()

    barrier = pltpu.get_barrier_semaphore()

    def greet(target):
        pl.semaphore_signal(barrier, inc=1, device_id={"ctx": target}, device_id_type=pl.DeviceIdType.MESH)

    pair, side = lax.div(me, 2), lax.rem(me, 2)

    @pl.when(me > 0)
    def _():
        greet(me - 1)

    greet(me + 1 - 2 * side)

    def greet_like(i, _):
        greet(2 * i + side)
        return 0

    lax.fori_loop(0, pair, greet_like, 0)
    for d in range(1, m):
        pl.semaphore_signal(
            barrier, inc=1, device_id={"tp": lax.rem(lane_rank + d, m)}, device_id_type=pl.DeviceIdType.MESH
        )

    loads[0].wait()
    rim_k = rim[0].astype(jnp.float32)[SUB:]
    rim_v = rim[1].astype(jnp.float32)[SUB:]
    send_kv[...] = jnp.concatenate([rim_k, rim_v], 0).astype(jnp.bfloat16)
    def columns(t):
        return pl.ds(pl.multiple_of(t * LANES, LANES), LANES)

    def tree(terms):
        while len(terms) > 1:
            terms = [a + b for a, b in zip(terms[::2], terms[1::2])] + terms[len(terms) // 2 * 2 :]
        return terms[0]

    def rounded(a):
        return a.astype(jnp.bfloat16).astype(jnp.float32)

    sub = lax.broadcasted_iota(jnp.int32, (SUB, LANES), 0).astype(jnp.float32)
    scale = 1.0 / math.sqrt(length)
    for i in (1, 2):
        loads[i].wait()
    rate_all = rates[...]
    a1[...] = jnp.exp(-rate_all / length)
    a8[...] = jnp.exp(-(rate_all * SUB) / length)
    a120[...] = jnp.exp(-(rate_all * (rows - SUB)) / length)
    a128[...] = jnp.exp(-(rate_all * rows) / length)

    def body_c(t, _):
        cols = columns(t)
        step = [jnp.broadcast_to(a8[i : i + 1, cols], (SUB, LANES)) for i in range(modes)]
        w = []
        for i in range(modes):
            r = rates[i : i + 1, cols]
            rest = jnp.exp(-(r * (SUB - 1 - sub)) / length)
            state[i, t] = rest
            state0[i, t] = rest * a120[i : i + 1, cols]
            here = (res[i : i + 1, cols] * scale) * jnp.exp(-(r * sub) / length)
            w.append(here)
            tailw[i, t] = here * a1[i : i + 1, cols]
        for b in range(0, blocks, 2):
            first = tree(w)
            w = [w[i] * step[i] for i in range(modes)]
            both = jnp.concatenate([first, tree(w)], 0)
            if b < blocks - 2:
                w = [w[i] * step[i] for i in range(modes)]
            hi = both.astype(jnp.bfloat16)
            lo = (both - hi.astype(jnp.float32)).astype(jnp.bfloat16)
            filt[pl.ds(b * SUB, 2 * SUB), cols] = hi
            filt[pl.ds(rows + b * SUB, 2 * SUB), cols] = hi
            filt[pl.ds(2 * rows + b * SUB, 2 * SUB), cols] = lo
        return 0

    lax.fori_loop(0, tiles, body_c, 0)
    pl.semaphore_wait(barrier, jnp.where(me < n - 1, 1, 0) + 1 + (n // 2 - 1 - pair) + m - 1)

    def halo_copies():
        right = lax.rem(me + 1, n)
        first = pltpu.make_async_remote_copy(
            src_ref=send_kv, dst_ref=halo_kv, send_sem=halo_send.at[0], recv_sem=halo_recv.at[0],
            device_id={"ctx": right}, device_id_type=pl.DeviceIdType.MESH,
        )
        second = pltpu.make_async_remote_copy(
            src_ref=proj_h.at[0, pl.ds(rows - 16, 16)], dst_ref=halo_q, send_sem=halo_send.at[1],
            recv_sem=halo_recv.at[1], device_id={"ctx": right}, device_id_type=pl.DeviceIdType.MESH,
        )
        return first, second

    @pl.when(me < n - 1)
    def _():
        first, second = halo_copies()
        first.start()
        second.start()

    def short(g, t, start, count):
        cols = slice(t * LANES, (t + 1) * LANES) if isinstance(t, int) else columns(t)
        total = None
        for j in range(taps_n):
            term = taps[g, j : j + 1, cols] * x[g, t, pl.ds(SUB + start - j, count), :]
            total = term if total is None else total + term
        return total

    def body_a(t, _):
        cols = columns(t)
        for g in (1, 2):
            x[g, t, pl.ds(SUB, rows), :] = proj[g, :, cols].astype(jnp.float32)
        kv[t, pl.ds(SUB, rows - SUB), :] = rounded(
            short(1, t, SUB, rows - SUB) * short(2, t, SUB, rows - SUB)
        )
        step = [jnp.broadcast_to(a8[i : i + 1, cols], (SUB, LANES)) for i in range(modes)]
        s = [kv[t, pl.ds(SUB, SUB), :]] * modes
        for b in range(2, blocks):
            u = kv[t, pl.ds(b * SUB, SUB), :]
            s = [step[i] * s[i] + u for i in range(modes)]
        for i in range(modes):
            state[i, t] = s[i] * state[i, t]
        return 0

    for i in (3, 4):
        loads[i].wait()
    lax.fori_loop(0, tiles, body_a, 0)

    @pl.when(me > 0)
    def _():
        first, _second = halo_copies()
        first.wait_recv()
        tail = halo_kv[...].astype(jnp.float32)
        for t in range(tiles):
            x[1, t, pl.ds(0, SUB), :] = tail[:SUB, t * LANES : (t + 1) * LANES]
            x[2, t, pl.ds(0, SUB), :] = tail[SUB:, t * LANES : (t + 1) * LANES]

    @pl.when(me == 0)
    def _():
        for g in range(3):
            for t in range(tiles):
                x[g, t, pl.ds(0, SUB), :] = jnp.zeros((SUB, LANES), jnp.float32)

    for t in range(tiles):
        cols = slice(t * LANES, (t + 1) * LANES)
        u = rounded(short(1, t, 0, SUB) * short(2, t, 0, SUB))
        kv[t, pl.ds(0, SUB), :] = u
        for i in range(modes):
            end_f[i : i + 1, cols] = jnp.sum(state[i, t] + state0[i, t] * u, axis=0, keepdims=True)
    end_b[...] = end_f[...].astype(jnp.bfloat16)

    mate = me + 1 - 2 * lax.rem(me, 2)
    pairs_n = n // 2

    mate_copy = pltpu.make_async_remote_copy(
        src_ref=end_b, dst_ref=mate_b, send_sem=mate_sem.at[0], recv_sem=mate_sem.at[1],
        device_id={"ctx": mate}, device_id_type=pl.DeviceIdType.MESH,
    )
    mate_copy.start()

    def end_copy(slot, target):
        return pltpu.make_async_remote_copy(
            src_ref=pair_b, dst_ref=ends.at[slot], send_sem=end_send.at[target], recv_sem=end_recv.at[slot],
            device_id={"ctx": 2 * target + side}, device_id_type=pl.DeviceIdType.MESH,
        )

    def send_end(j, _):
        end_copy(pair, j).start()
        return 0

    for i in range(5, len(loads)):
        loads[i].wait()

    width = 2 * LANES
    groups = [slice(c, c + width) for c in range(0, channels, width)]
    for c in groups:
        t0 = c.start // LANES
        u = jnp.concatenate([kv[t0], kv[t0 + 1]], 1).astype(jnp.bfloat16)
        spec_f[:, c] = dot(fwd[...], filt[:, c])
        spec_u[:, c] = dot(fwd[:, : 2 * rows], jnp.concatenate([u, u], 0))
    mate_copy.wait_recv()
    other = mate_b[...].astype(jnp.float32)
    early = jnp.where(side == 0, end_f[...], other)
    late = jnp.where(side == 0, other, end_f[...])
    pair_b[...] = (early * a128[...] + late).astype(jnp.bfloat16)
    lax.fori_loop(pair + 1, pairs_n, send_end, 0)

    for c in groups:
        ur, ui, fr, fi = spec_u[:rows, c], spec_u[rows:, c], spec_f[:rows, c], spec_f[rows:, c]
        for at, part in ((0, ur * fr - ui * fi), (rows, ur * fi + ui * fr)):
            hi = part.astype(jnp.bfloat16)
            prod_hi[at : at + rows, c] = hi
            prod_lo[at : at + rows, c] = (part - hi.astype(jnp.float32)).astype(jnp.bfloat16)
    for c in groups:
        t0 = c.start // LANES
        y = dot(inv[...], prod_hi[:, c])
        y = y[:rows] + y[rows:] + dot(inv[:rows], prod_lo[:, c])
        long[t0] = y[:, :LANES]
        long[t0 + 1] = y[:, LANES:]

    @pl.when(me > 0)
    def _():
        _first, second = halo_copies()
        second.wait_recv()
        tail = halo_q[...].astype(jnp.float32)[SUB:]
        for t in range(tiles):
            x[0, t, pl.ds(0, SUB), :] = tail[:, t * LANES : (t + 1) * LANES]

    def body_q(t, _):
        x[0, t, pl.ds(SUB, rows), :] = proj[0, :, columns(t)].astype(jnp.float32)
        gated[t] = short(0, t, 0, rows)
        return 0

    lax.fori_loop(0, tiles, body_q, 0)

    def gather(i, carry):
        end_copy(i, i).wait_recv()
        return carry * (a128[...] * a128[...]) + ends[i].astype(jnp.float32)

    carry = lax.fori_loop(0, pair, gather, jnp.zeros((modes, channels), jnp.float32))
    end_f[...] = jnp.where(side == 0, carry, carry * a128[...] + mate_b[...].astype(jnp.float32))
    squares[...] = jnp.zeros_like(squares)

    def body_e(t, _):
        cols = columns(t)
        step = [jnp.broadcast_to(a8[i : i + 1, cols], (SUB, LANES)) for i in range(modes)]
        w = [tailw[i, t] * end_f[i : i + 1, cols] for i in range(modes)]
        direct = skip[:, cols]
        for b in range(blocks):
            here = pl.ds(b * SUB, SUB)
            y = rounded(long[t, here, :] + tree(w))
            g = gated[t, here, :] * (y + direct * kv[t, here, :])
            gated[t, here, :] = g
            squares[here, :] += g * g
            if b < blocks - 1:
                w = [w[i] * step[i] for i in range(modes)]
        return 0

    lax.fori_loop(0, tiles, body_e, 0)

    def halves(a, axis):
        hi = a.astype(jnp.bfloat16)
        return jnp.concatenate([hi, (a - hi.astype(jnp.float32)).astype(jnp.bfloat16)], axis)

    mine = lax.dot_general(
        jnp.ones((2 * SUB, 2 * LANES), jnp.bfloat16), halves(squares[...], 1), (((1,), (1,)), ((), ())),
        preferred_element_type=jnp.float32,
    )[:SUB]
    sums[lane_rank] = mine

    def sum_copy(d, slot):
        return pltpu.make_async_remote_copy(
            src_ref=sums.at[lane_rank], dst_ref=sums.at[slot], send_sem=sum_send.at[d],
            recv_sem=sum_recv.at[slot], device_id={"tp": lax.rem(lane_rank + d, m)},
            device_id_type=pl.DeviceIdType.MESH,
        )

    for d in range(1, m):
        sum_copy(d, lane_rank).start()
    for d in range(1, m):
        sum_copy(d, lax.rem(lane_rank + d, m)).wait_recv()
    total = sums[0]
    for d in range(1, m):
        total = total + sums[d]
    inverse = 1.0 / jnp.sqrt(total / (channels * m) + 1e-05)
    spread = lax.dot_general(
        halves(inverse, 0), jnp.full((2 * SUB, LANES), 1.0 / SUB, jnp.bfloat16), (((0,), (0,)), ((), ())),
        preferred_element_type=jnp.float32,
    )

    for t in range(tiles):
        cols = slice(t * LANES, (t + 1) * LANES)
        out[:, cols] = (gated[t] * gain[:, cols] * spread).astype(jnp.bfloat16)

    @pl.when(me < n - 1)
    def _():
        first, second = halo_copies()
        first.wait_send()
        second.wait_send()

    def finish(j, _):
        end_copy(pair, j).wait_send()
        return 0

    lax.fori_loop(pair + 1, pairs_n, finish, 0)
    mate_copy.wait_send()
    for d in range(1, m):
        sum_copy(d, lane_rank).wait_send()


def solution(mesh):
    n, m = mesh.shape["ctx"], mesh.shape["tp"]

    def shards(projected, short_taps, residues, rates, skip_gain, norm_gain):
        rows, _, channels = projected.shape
        modes = rates.shape[1]
        tiles = channels // LANES
        f32, bf16 = jnp.float32, jnp.bfloat16
        fwd, inv = (jnp.asarray(a) for a in tables(rows))
        tile3 = pltpu.VMEM((tiles, rows, LANES), f32)
        modal = pltpu.VMEM((modes, tiles, SUB, LANES), f32)
        flat = pltpu.VMEM((modes, channels), f32)
        dma = pltpu.SemaphoreType.DMA
        return pl.pallas_call(
            functools.partial(kernel, n, m, modes, short_taps.shape[1], rows, channels, rows * n),
            out_shape=jax.ShapeDtypeStruct((rows, channels), bf16),
            in_specs=[pl.BlockSpec(memory_space=pltpu.HBM)] * 8,
            out_specs=pl.BlockSpec(memory_space=pltpu.VMEM),
            scratch_shapes=[
                pltpu.VMEM((2, 16, channels), bf16),
                pltpu.VMEM(projected.shape[1:2] + (rows, channels), bf16),
                pltpu.VMEM(short_taps.shape, f32), flat, flat,
                pltpu.VMEM((1, channels), f32), pltpu.VMEM((1, channels), f32),
                pltpu.VMEM(fwd.shape, bf16), pltpu.VMEM(inv.shape, bf16),
                dma((10,)),
                flat, flat,
                pltpu.VMEM((3, tiles, rows + SUB, LANES), f32),
                tile3, modal, modal,
                pltpu.VMEM((3 * rows, channels), bf16),
                pltpu.VMEM((2 * rows, channels), f32), pltpu.VMEM((2 * rows, channels), f32),
                pltpu.VMEM((2 * rows, channels), bf16), pltpu.VMEM((2 * rows, channels), bf16),
                modal, flat, flat, tile3, tile3,
                pltpu.VMEM((rows, LANES), f32),
                pltpu.VMEM((16, channels), bf16),
                pltpu.VMEM((16, channels), bf16),
                pltpu.VMEM((16, channels), bf16),
                flat,
                pltpu.VMEM((modes, channels), bf16),
                pltpu.VMEM((modes, channels), bf16),
                pltpu.VMEM((modes, channels), bf16),
                pltpu.VMEM((n // 2, modes, channels), bf16),
                pltpu.VMEM((m, SUB, LANES), f32),
                dma((2,)), dma((2,)), dma((n // 2,)), dma((n // 2,)), dma((m,)), dma((m,)), dma((2,)),
            ],
            compiler_params=pltpu.CompilerParams(
                collective_id=0, has_side_effects=True, vmem_limit_bytes=32 * 1024 * 1024
            ),
        )(*(
            pltpu.with_memory_space_constraint(a, pltpu.HBM)
            for a in (
                jnp.transpose(projected, (1, 0, 2)), short_taps, residues.T, rates.T,
                skip_gain[None, :], norm_gain[None, :], fwd, inv,
            )
        ))

    return jax.shard_map(
        shards,
        mesh=mesh,
        in_specs=(
            P("ctx", None, "tp"),
            P(None, None, "tp"),
            P("tp", None),
            P("tp", None),
            P("tp"),
            P("tp"),
        ),
        out_specs=P("ctx", "tp"),
        check_vma=False,
    )
```

```python
import functools
import math

import jax
import jax.numpy as jnp
import ml_dtypes
import numpy as np
from jax import lax
from jax.experimental import pallas as pl
from jax.experimental.pallas import tpu as pltpu
from jax.sharding import PartitionSpec as P

LANES = 128
SUB = 8


def tables(rows):
    freq = (np.arange(rows) + 0.5)[:, None] * (2.0 * math.pi / (2 * rows))
    angle = freq * np.arange(rows)[None, :]
    forward = np.concatenate([np.cos(angle), -np.sin(angle)], 0)
    inverse = forward.T / rows

    def pair(a):
        hi = a.astype(ml_dtypes.bfloat16)
        lo = (a - hi.astype(np.float64)).astype(ml_dtypes.bfloat16)
        return hi, lo

    f_hi, f_lo = pair(forward)
    g_hi, g_lo = pair(inverse)
    return np.concatenate([f_hi, f_lo, f_hi], 1), np.concatenate([g_hi, g_lo], 0)


def kernel(
    n, m, modes, taps_n, rows, channels, length,
    proj_h, taps_h, res_h, rates_h, skip_h, gain_h, fwd_h, inv_h,
    out,
    rim, proj, taps, res, rates, skip, gain, fwd, inv, load_sem,
    a1, a120, x, kv, state, state0, filt, spec_f, spec_u, prod_hi, prod_lo, tailw, a8, a128, long, gated, squares,
    send_kv, halo_kv, halo_q, end_f, end_b, mate_b, pair_b, ends, sums,
    halo_send, halo_recv, end_send, end_recv, sum_send, sum_recv, mate_sem,
):
    me = lax.axis_index("ctx")
    lane_rank = lax.axis_index("tp")
    tiles = channels // LANES
    blocks = rows // SUB
    dot = functools.partial(jnp.dot, preferred_element_type=jnp.float32)

    pairs = [
        (proj_h.at[pl.ds(1, 2), pl.ds(rows - 16, 16)], rim),
        (rates_h, rates), (res_h, res), (taps_h, taps),
        (proj_h.at[pl.ds(1, 2)], proj.at[pl.ds(1, 2)]),
        (proj_h.at[0], proj.at[0]),
        (fwd_h, fwd), (inv_h, inv), (skip_h, skip), (gain_h, gain),
    ]
    loads = [pltpu.make_async_copy(a, b, load_sem.at[i]) for i, (a, b) in enumerate(pairs)]
    for load in loads:
        load.start()

    barrier = pltpu.get_barrier_semaphore()

    def greet(target):
        pl.semaphore_signal(barrier, inc=1, device_id={"ctx": target}, device_id_type=pl.DeviceIdType.MESH)

    pair, side = lax.div(me, 2), lax.rem(me, 2)

    @pl.when(me > 0)
    def _():
        greet(me - 1)

    greet(me + 1 - 2 * side)

    def greet_like(i, _):
        greet(2 * i + side)
        return 0

    lax.fori_loop(0, pair, greet_like, 0)
    for d in range(1, m):
        pl.semaphore_signal(
            barrier, inc=1, device_id={"tp": lax.rem(lane_rank + d, m)}, device_id_type=pl.DeviceIdType.MESH
        )

    loads[0].wait()
    rim_k = rim[0].astype(jnp.float32)[SUB:]
    rim_v = rim[1].astype(jnp.float32)[SUB:]
    send_kv[...] = jnp.concatenate([rim_k, rim_v], 0).astype(jnp.bfloat16)
    def columns(t):
        return pl.ds(pl.multiple_of(t * LANES, LANES), LANES)

    def tree(terms):
        while len(terms) > 1:
            terms = [a + b for a, b in zip(terms[::2], terms[1::2])] + terms[len(terms) // 2 * 2 :]
        return terms[0]

    def rounded(a):
        return a.astype(jnp.bfloat16).astype(jnp.float32)

    sub = lax.broadcasted_iota(jnp.int32, (SUB, LANES), 0)
    odd, second, third = (sub & 1) > 0, (sub & 2) > 0, (sub & 4) > 0
    scale = 1.0 / math.sqrt(length)
    for i in (1, 2):
        loads[i].wait()
    rate_all = rates[...]
    a1[...] = jnp.exp(-rate_all / length)
    a8[...] = jnp.exp(-(rate_all * SUB) / length)
    a120[...] = jnp.exp(-(rate_all * (rows - SUB)) / length)
    a128[...] = jnp.exp(-(rate_all * rows) / length)

    def body_c(t, _):
        cols = columns(t)
        step = [jnp.broadcast_to(a8[i : i + 1, cols], (SUB, LANES)) for i in range(modes)]
        w = []
        for i in range(modes):
            one = a1[i : i + 1, cols]
            two = one * one
            four = two * two
            rest = jnp.where(odd, 1.0, one) * jnp.where(second, 1.0, two) * jnp.where(third, 1.0, four)
            past = jnp.where(odd, one, 1.0) * jnp.where(second, two, 1.0) * jnp.where(third, four, 1.0)
            state[i, t] = rest
            state0[i, t] = rest * a120[i : i + 1, cols]
            here = (res[i : i + 1, cols] * scale) * past
            w.append(here)
            tailw[i, t] = here * one
        for b in range(0, blocks, 2):
            first = tree(w)
            w = [w[i] * step[i] for i in range(modes)]
            both = jnp.concatenate([first, tree(w)], 0)
            if b < blocks - 2:
                w = [w[i] * step[i] for i in range(modes)]
            hi = both.astype(jnp.bfloat16)
            lo = (both - hi.astype(jnp.float32)).astype(jnp.bfloat16)
            filt[pl.ds(b * SUB, 2 * SUB), cols] = hi
            filt[pl.ds(rows + b * SUB, 2 * SUB), cols] = hi
            filt[pl.ds(2 * rows + b * SUB, 2 * SUB), cols] = lo
        return 0

    lax.fori_loop(0, tiles, body_c, 0)
    pl.semaphore_wait(barrier, jnp.where(me < n - 1, 1, 0) + 1 + (n // 2 - 1 - pair) + m - 1)

    def halo_copies():
        right = lax.rem(me + 1, n)
        first = pltpu.make_async_remote_copy(
            src_ref=send_kv, dst_ref=halo_kv, send_sem=halo_send.at[0], recv_sem=halo_recv.at[0],
            device_id={"ctx": right}, device_id_type=pl.DeviceIdType.MESH,
        )
        second = pltpu.make_async_remote_copy(
            src_ref=proj_h.at[0, pl.ds(rows - 16, 16)], dst_ref=halo_q, send_sem=halo_send.at[1],
            recv_sem=halo_recv.at[1], device_id={"ctx": right}, device_id_type=pl.DeviceIdType.MESH,
        )
        return first, second

    @pl.when(me < n - 1)
    def _():
        first, second = halo_copies()
        first.start()
        second.start()

    def short(g, t, start, count):
        cols = slice(t * LANES, (t + 1) * LANES) if isinstance(t, int) else columns(t)
        total = None
        for j in range(taps_n):
            term = taps[g, j : j + 1, cols] * x[g, t, pl.ds(SUB + start - j, count), :]
            total = term if total is None else total + term
        return total

    def body_a(t, _):
        cols = columns(t)
        for g in (1, 2):
            x[g, t, pl.ds(SUB, rows), :] = proj[g, :, cols].astype(jnp.float32)
        kv[t, pl.ds(SUB, rows - SUB), :] = rounded(
            short(1, t, SUB, rows - SUB) * short(2, t, SUB, rows - SUB)
        )
        step = [jnp.broadcast_to(a8[i : i + 1, cols], (SUB, LANES)) for i in range(modes)]
        s = [kv[t, pl.ds(SUB, SUB), :]] * modes
        for b in range(2, blocks):
            u = kv[t, pl.ds(b * SUB, SUB), :]
            s = [step[i] * s[i] + u for i in range(modes)]
        for i in range(modes):
            state[i, t] = s[i] * state[i, t]
        return 0

    for i in (3, 4):
        loads[i].wait()
    lax.fori_loop(0, tiles, body_a, 0)

    @pl.when(me > 0)
    def _():
        first, _second = halo_copies()
        first.wait_recv()
        tail = halo_kv[...].astype(jnp.float32)
        for t in range(tiles):
            x[1, t, pl.ds(0, SUB), :] = tail[:SUB, t * LANES : (t + 1) * LANES]
            x[2, t, pl.ds(0, SUB), :] = tail[SUB:, t * LANES : (t + 1) * LANES]

    @pl.when(me == 0)
    def _():
        for g in range(3):
            for t in range(tiles):
                x[g, t, pl.ds(0, SUB), :] = jnp.zeros((SUB, LANES), jnp.float32)

    for t in range(tiles):
        cols = slice(t * LANES, (t + 1) * LANES)
        u = rounded(short(1, t, 0, SUB) * short(2, t, 0, SUB))
        kv[t, pl.ds(0, SUB), :] = u
        for i in range(modes):
            end_f[i : i + 1, cols] = jnp.sum(state[i, t] + state0[i, t] * u, axis=0, keepdims=True)
    end_b[...] = end_f[...].astype(jnp.bfloat16)

    mate = me + 1 - 2 * lax.rem(me, 2)
    pairs_n = n // 2

    mate_copy = pltpu.make_async_remote_copy(
        src_ref=end_b, dst_ref=mate_b, send_sem=mate_sem.at[0], recv_sem=mate_sem.at[1],
        device_id={"ctx": mate}, device_id_type=pl.DeviceIdType.MESH,
    )
    mate_copy.start()

    def end_copy(slot, target):
        return pltpu.make_async_remote_copy(
            src_ref=pair_b, dst_ref=ends.at[slot], send_sem=end_send.at[target], recv_sem=end_recv.at[slot],
            device_id={"ctx": 2 * target + side}, device_id_type=pl.DeviceIdType.MESH,
        )

    def send_end(j, _):
        end_copy(pair, j).start()
        return 0

    for i in range(5, len(loads)):
        loads[i].wait()

    width = 2 * LANES
    groups = [slice(c, c + width) for c in range(0, channels, width)]
    for c in groups:
        t0 = c.start // LANES
        u = jnp.concatenate([kv[t0], kv[t0 + 1]], 1).astype(jnp.bfloat16)
        spec_f[:, c] = dot(fwd[...], filt[:, c])
        spec_u[:, c] = dot(fwd[:, : 2 * rows], jnp.concatenate([u, u], 0))
    mate_copy.wait_recv()
    other = mate_b[...].astype(jnp.float32)
    early = jnp.where(side == 0, end_f[...], other)
    late = jnp.where(side == 0, other, end_f[...])
    pair_b[...] = (early * a128[...] + late).astype(jnp.bfloat16)
    lax.fori_loop(pair + 1, pairs_n, send_end, 0)

    for c in groups:
        ur, ui, fr, fi = spec_u[:rows, c], spec_u[rows:, c], spec_f[:rows, c], spec_f[rows:, c]
        for at, part in ((0, ur * fr - ui * fi), (rows, ur * fi + ui * fr)):
            hi = part.astype(jnp.bfloat16)
            prod_hi[at : at + rows, c] = hi
            prod_lo[at : at + rows, c] = (part - hi.astype(jnp.float32)).astype(jnp.bfloat16)
    for c in groups:
        t0 = c.start // LANES
        y = dot(inv[...], prod_hi[:, c])
        y = y[:rows] + y[rows:] + dot(inv[:rows], prod_lo[:, c])
        long[t0] = y[:, :LANES]
        long[t0 + 1] = y[:, LANES:]

    @pl.when(me > 0)
    def _():
        _first, second = halo_copies()
        second.wait_recv()
        tail = halo_q[...].astype(jnp.float32)[SUB:]
        for t in range(tiles):
            x[0, t, pl.ds(0, SUB), :] = tail[:, t * LANES : (t + 1) * LANES]

    def body_q(t, _):
        x[0, t, pl.ds(SUB, rows), :] = proj[0, :, columns(t)].astype(jnp.float32)
        gated[t] = short(0, t, 0, rows)
        return 0

    lax.fori_loop(0, tiles, body_q, 0, unroll=2)

    def gather(i, carry):
        end_copy(i, i).wait_recv()
        return carry * (a128[...] * a128[...]) + ends[i].astype(jnp.float32)

    carry = lax.fori_loop(0, pair, gather, jnp.zeros((modes, channels), jnp.float32))
    end_f[...] = jnp.where(side == 0, carry, carry * a128[...] + mate_b[...].astype(jnp.float32))
    squares[...] = jnp.zeros_like(squares)

    def body_e(t, _):
        cols = columns(t)
        step = [jnp.broadcast_to(a8[i : i + 1, cols], (SUB, LANES)) for i in range(modes)]
        w = [tailw[i, t] * end_f[i : i + 1, cols] for i in range(modes)]
        direct = skip[:, cols]
        for b in range(blocks):
            here = pl.ds(b * SUB, SUB)
            y = rounded(long[t, here, :] + tree(w))
            g = gated[t, here, :] * (y + direct * kv[t, here, :])
            gated[t, here, :] = g
            squares[here, :] += g * g
            if b < blocks - 1:
                w = [w[i] * step[i] for i in range(modes)]
        return 0

    lax.fori_loop(0, tiles, body_e, 0)

    def halves(a, axis):
        hi = a.astype(jnp.bfloat16)
        return jnp.concatenate([hi, (a - hi.astype(jnp.float32)).astype(jnp.bfloat16)], axis)

    mine = lax.dot_general(
        jnp.ones((2 * SUB, 2 * LANES), jnp.bfloat16), halves(squares[...], 1), (((1,), (1,)), ((), ())),
        preferred_element_type=jnp.float32,
    )[:SUB]
    sums[lane_rank] = mine

    def sum_copy(d, slot):
        return pltpu.make_async_remote_copy(
            src_ref=sums.at[lane_rank], dst_ref=sums.at[slot], send_sem=sum_send.at[d],
            recv_sem=sum_recv.at[slot], device_id={"tp": lax.rem(lane_rank + d, m)},
            device_id_type=pl.DeviceIdType.MESH,
        )

    for d in range(1, m):
        sum_copy(d, lane_rank).start()
    for d in range(1, m):
        sum_copy(d, lax.rem(lane_rank + d, m)).wait_recv()
    total = sums[0]
    for d in range(1, m):
        total = total + sums[d]
    inverse = 1.0 / jnp.sqrt(total / (channels * m) + 1e-05)
    spread = lax.dot_general(
        halves(inverse, 0), jnp.full((2 * SUB, LANES), 1.0 / SUB, jnp.bfloat16), (((0,), (0,)), ((), ())),
        preferred_element_type=jnp.float32,
    )

    for t in range(tiles):
        cols = slice(t * LANES, (t + 1) * LANES)
        out[:, cols] = (gated[t] * gain[:, cols] * spread).astype(jnp.bfloat16)

    @pl.when(me < n - 1)
    def _():
        first, second = halo_copies()
        first.wait_send()
        second.wait_send()

    def finish(j, _):
        end_copy(pair, j).wait_send()
        return 0

    lax.fori_loop(pair + 1, pairs_n, finish, 0)
    mate_copy.wait_send()
    for d in range(1, m):
        sum_copy(d, lane_rank).wait_send()


def solution(mesh):
    n, m = mesh.shape["ctx"], mesh.shape["tp"]

    def shards(projected, short_taps, residues, rates, skip_gain, norm_gain):
        rows, _, channels = projected.shape
        modes = rates.shape[1]
        tiles = channels // LANES
        f32, bf16 = jnp.float32, jnp.bfloat16
        fwd, inv = (jnp.asarray(a) for a in tables(rows))
        tile3 = pltpu.VMEM((tiles, rows, LANES), f32)
        modal = pltpu.VMEM((modes, tiles, SUB, LANES), f32)
        flat = pltpu.VMEM((modes, channels), f32)
        dma = pltpu.SemaphoreType.DMA
        return pl.pallas_call(
            functools.partial(kernel, n, m, modes, short_taps.shape[1], rows, channels, rows * n),
            out_shape=jax.ShapeDtypeStruct((rows, channels), bf16),
            in_specs=[pl.BlockSpec(memory_space=pltpu.HBM)] * 8,
            out_specs=pl.BlockSpec(memory_space=pltpu.VMEM),
            scratch_shapes=[
                pltpu.VMEM((2, 16, channels), bf16),
                pltpu.VMEM(projected.shape[1:2] + (rows, channels), bf16),
                pltpu.VMEM(short_taps.shape, f32), flat, flat,
                pltpu.VMEM((1, channels), f32), pltpu.VMEM((1, channels), f32),
                pltpu.VMEM(fwd.shape, bf16), pltpu.VMEM(inv.shape, bf16),
                dma((10,)),
                flat, flat,
                pltpu.VMEM((3, tiles, rows + SUB, LANES), f32),
                tile3, modal, modal,
                pltpu.VMEM((3 * rows, channels), bf16),
                pltpu.VMEM((2 * rows, channels), f32), pltpu.VMEM((2 * rows, channels), f32),
                pltpu.VMEM((2 * rows, channels), bf16), pltpu.VMEM((2 * rows, channels), bf16),
                modal, flat, flat, tile3, tile3,
                pltpu.VMEM((rows, LANES), f32),
                pltpu.VMEM((16, channels), bf16),
                pltpu.VMEM((16, channels), bf16),
                pltpu.VMEM((16, channels), bf16),
                flat,
                pltpu.VMEM((modes, channels), bf16),
                pltpu.VMEM((modes, channels), bf16),
                pltpu.VMEM((modes, channels), bf16),
                pltpu.VMEM((n // 2, modes, channels), bf16),
                pltpu.VMEM((m, SUB, LANES), f32),
                dma((2,)), dma((2,)), dma((n // 2,)), dma((n // 2,)), dma((m,)), dma((m,)), dma((2,)),
            ],
            compiler_params=pltpu.CompilerParams(
                collective_id=0, has_side_effects=True, vmem_limit_bytes=32 * 1024 * 1024
            ),
        )(*(
            pltpu.with_memory_space_constraint(a, pltpu.HBM)
            for a in (
                jnp.transpose(projected, (1, 0, 2)), short_taps, residues.T, rates.T,
                skip_gain[None, :], norm_gain[None, :], fwd, inv,
            )
        ))

    return jax.shard_map(
        shards,
        mesh=mesh,
        in_specs=(
            P("ctx", None, "tp"),
            P(None, None, "tp"),
            P("tp", None),
            P("tp", None),
            P("tp"),
            P("tp"),
        ),
        out_specs=P("ctx", "tp"),
        check_vma=False,
    )
```

```python
import functools
import math

import jax
import jax.numpy as jnp
import ml_dtypes
import numpy as np
from jax import lax
from jax.experimental import pallas as pl
from jax.experimental.pallas import tpu as pltpu
from jax.sharding import PartitionSpec as P

LANES = 128
SUB = 8


def tables(rows):
    freq = (np.arange(rows) + 0.5)[:, None] * (2.0 * math.pi / (2 * rows))
    angle = freq * np.arange(rows)[None, :]
    forward = np.concatenate([np.cos(angle), -np.sin(angle)], 0)
    order = np.arange(rows).reshape(SUB, rows // SUB).T.reshape(-1)
    forward = forward[:, order]
    inverse = forward.T / rows

    def pair(a):
        hi = a.astype(ml_dtypes.bfloat16)
        lo = (a - hi.astype(np.float64)).astype(ml_dtypes.bfloat16)
        return hi, lo

    f_hi, f_lo = pair(forward)
    g_hi, g_lo = pair(inverse)
    return np.concatenate([f_hi, f_lo, f_hi], 1), np.concatenate([g_hi, g_lo], 0)


def kernel(
    n, m, modes, taps_n, rows, channels, length,
    proj_h, taps_h, res_h, rates_h, skip_h, gain_h, fwd_h, inv_h,
    out,
    rim, proj, taps, res, rates, skip, gain, fwd, inv, load_sem,
    a1, a16, x, kv, state, filt, spec_f, spec_u, prod_hi, prod_lo, tailw, a128, long, gated, squares,
    send_kv, halo_kv, halo_q, end_f, end_b, mate_b, pair_b, ends, sums,
    halo_send, halo_recv, end_send, end_recv, sum_send, sum_recv, mate_sem,
):
    me = lax.axis_index("ctx")
    lane_rank = lax.axis_index("tp")
    tiles = channels // LANES
    blocks = rows // SUB
    dot = functools.partial(jnp.dot, preferred_element_type=jnp.float32)

    pairs = [
        (proj_h.at[pl.ds(1, 2), pl.ds(rows - 16, 16)], rim),
        (rates_h, rates), (res_h, res), (taps_h, taps),
        (proj_h.at[pl.ds(1, 2)], proj.at[pl.ds(1, 2)]),
        (proj_h.at[0], proj.at[0]),
        (fwd_h, fwd), (inv_h, inv), (skip_h, skip), (gain_h, gain),
    ]
    loads = [pltpu.make_async_copy(a, b, load_sem.at[i]) for i, (a, b) in enumerate(pairs)]
    for load in loads:
        load.start()

    barrier = pltpu.get_barrier_semaphore()

    def greet(target):
        pl.semaphore_signal(barrier, inc=1, device_id={"ctx": target}, device_id_type=pl.DeviceIdType.MESH)

    pair, side = lax.div(me, 2), lax.rem(me, 2)

    @pl.when(me > 0)
    def _():
        greet(me - 1)

    greet(me + 1 - 2 * side)

    def greet_like(i, _):
        greet(2 * i + side)
        return 0

    lax.fori_loop(0, pair, greet_like, 0)
    for d in range(1, m):
        pl.semaphore_signal(
            barrier, inc=1, device_id={"tp": lax.rem(lane_rank + d, m)}, device_id_type=pl.DeviceIdType.MESH
        )

    loads[0].wait()
    rim_k = rim[0].astype(jnp.float32)[SUB:]
    rim_v = rim[1].astype(jnp.float32)[SUB:]
    send_kv[...] = jnp.concatenate([rim_k, rim_v], 0).astype(jnp.bfloat16)
    pl.semaphore_wait(barrier, jnp.where(me < n - 1, 1, 0) + 1 + (n // 2 - 1 - pair) + m - 1)

    def halo_copies():
        right = lax.rem(me + 1, n)
        first = pltpu.make_async_remote_copy(
            src_ref=send_kv, dst_ref=halo_kv, send_sem=halo_send.at[0], recv_sem=halo_recv.at[0],
            device_id={"ctx": right}, device_id_type=pl.DeviceIdType.MESH,
        )
        second = pltpu.make_async_remote_copy(
            src_ref=proj_h.at[0, pl.ds(rows - 16, 16)], dst_ref=halo_q, send_sem=halo_send.at[1],
            recv_sem=halo_recv.at[1], device_id={"ctx": right}, device_id_type=pl.DeviceIdType.MESH,
        )
        return first, second

    @pl.when(me < n - 1)
    def _():
        first, second = halo_copies()
        first.start()
        second.start()

    def columns(t):
        return pl.ds(pl.multiple_of(t * LANES, LANES), LANES)

    def tree(terms):
        while len(terms) > 1:
            terms = [a + b for a, b in zip(terms[::2], terms[1::2])] + terms[len(terms) // 2 * 2 :]
        return terms[0]

    def rounded(a):
        return a.astype(jnp.bfloat16).astype(jnp.float32)

    sub = lax.broadcasted_iota(jnp.int32, (SUB, LANES), 0)
    odd, second, third = (sub & 1) > 0, (sub & 2) > 0, (sub & 4) > 0
    scale = 1.0 / math.sqrt(length)
    for i in (1, 2):
        loads[i].wait()
    rate_all = rates[...]
    a1[...] = jnp.exp(-rate_all / length)
    a16[...] = jnp.exp(-(rate_all * blocks) / length)
    a128[...] = jnp.exp(-(rate_all * rows) / length)

    def body_c(t, _):
        cols = columns(t)
        step = [jnp.broadcast_to(a1[i : i + 1, cols], (SUB, LANES)) for i in range(modes)]
        w = []
        for i in range(modes):
            one = a16[i : i + 1, cols]
            two = one * one
            four = two * two
            rest = jnp.where(odd, 1.0, one) * jnp.where(second, 1.0, two) * jnp.where(third, 1.0, four)
            past = jnp.where(odd, one, 1.0) * jnp.where(second, two, 1.0) * jnp.where(third, four, 1.0)
            state[i, t] = rest
            here = (res[i : i + 1, cols] * scale) * past
            w.append(here)
            tailw[i, t] = here * a1[i : i + 1, cols]
        for b in range(0, blocks, 2):
            first = tree(w)
            w = [w[i] * step[i] for i in range(modes)]
            both = jnp.concatenate([first, tree(w)], 0)
            if b < blocks - 2:
                w = [w[i] * step[i] for i in range(modes)]
            hi = both.astype(jnp.bfloat16)
            lo = (both - hi.astype(jnp.float32)).astype(jnp.bfloat16)
            filt[pl.ds(b * SUB, 2 * SUB), cols] = hi
            filt[pl.ds(rows + b * SUB, 2 * SUB), cols] = hi
            filt[pl.ds(2 * rows + b * SUB, 2 * SUB), cols] = lo
        return 0

    lax.fori_loop(0, tiles, body_c, 0)
    def short(g, t):
        cols = columns(t)
        tap = [jnp.broadcast_to(taps[g, j : j + 1, cols], (SUB, LANES)) for j in range(taps_n)]
        x[g, t, pl.ds(SUB, rows), :] = proj[g, :, cols].astype(jnp.float32)
        shifted = {
            k: x[g, t, pl.ds(SUB + k, SUB, stride=blocks), :] for k in range(1 - taps_n, blocks)
        }
        return [tree([tap[j] * shifted[k - j] for j in range(taps_n)]) for k in range(blocks)]

    def body_a(t, _):
        cols = columns(t)
        u = [rounded(a * b) for a, b in zip(short(1, t), short(2, t))]
        step = [jnp.broadcast_to(a1[i : i + 1, cols], (SUB, LANES)) for i in range(modes)]
        s = [u[0]] * modes
        kv[t, pl.ds(0, SUB), :] = u[0]
        for b in range(1, blocks):
            kv[t, pl.ds(b * SUB, SUB), :] = u[b]
            s = [step[i] * s[i] + u[b] for i in range(modes)]
        for i in range(modes):
            end_f[i : i + 1, cols] = jnp.sum(s[i] * state[i, t], axis=0, keepdims=True)
        return 0

    for i in (3, 4):
        loads[i].wait()
    @pl.when(me > 0)
    def _():
        first, _second = halo_copies()
        first.wait_recv()
        tail = halo_kv[...].astype(jnp.float32)
        for t in range(tiles):
            x[1, t, pl.ds(0, SUB), :] = tail[:SUB, t * LANES : (t + 1) * LANES]
            x[2, t, pl.ds(0, SUB), :] = tail[SUB:, t * LANES : (t + 1) * LANES]

    @pl.when(me == 0)
    def _():
        for g in range(3):
            for t in range(tiles):
                x[g, t, pl.ds(0, SUB), :] = jnp.zeros((SUB, LANES), jnp.float32)

    lax.fori_loop(0, tiles, body_a, 0)
    end_b[...] = end_f[...].astype(jnp.bfloat16)

    mate = me + 1 - 2 * lax.rem(me, 2)
    pairs_n = n // 2

    mate_copy = pltpu.make_async_remote_copy(
        src_ref=end_b, dst_ref=mate_b, send_sem=mate_sem.at[0], recv_sem=mate_sem.at[1],
        device_id={"ctx": mate}, device_id_type=pl.DeviceIdType.MESH,
    )
    mate_copy.start()

    def end_copy(slot, target):
        return pltpu.make_async_remote_copy(
            src_ref=pair_b, dst_ref=ends.at[slot], send_sem=end_send.at[target], recv_sem=end_recv.at[slot],
            device_id={"ctx": 2 * target + side}, device_id_type=pl.DeviceIdType.MESH,
        )

    def send_end(j, _):
        end_copy(pair, j).start()
        return 0

    for i in range(5, len(loads)):
        loads[i].wait()

    width = 2 * LANES
    groups = [slice(c, c + width) for c in range(0, channels, width)]
    for c in groups:
        t0 = c.start // LANES
        u = jnp.concatenate([kv[t0], kv[t0 + 1]], 1).astype(jnp.bfloat16)
        spec_f[:, c] = dot(fwd[...], filt[:, c])
        spec_u[:, c] = dot(fwd[:, : 2 * rows], jnp.concatenate([u, u], 0))
    mate_copy.wait_recv()
    other = mate_b[...].astype(jnp.float32)
    early = jnp.where(side == 0, end_f[...], other)
    late = jnp.where(side == 0, other, end_f[...])
    pair_b[...] = (early * a128[...] + late).astype(jnp.bfloat16)
    lax.fori_loop(pair + 1, pairs_n, send_end, 0)

    for c in groups:
        ur, ui, fr, fi = spec_u[:rows, c], spec_u[rows:, c], spec_f[:rows, c], spec_f[rows:, c]
        for at, part in ((0, ur * fr - ui * fi), (rows, ur * fi + ui * fr)):
            hi = part.astype(jnp.bfloat16)
            prod_hi[at : at + rows, c] = hi
            prod_lo[at : at + rows, c] = (part - hi.astype(jnp.float32)).astype(jnp.bfloat16)
    for c in groups:
        t0 = c.start // LANES
        y = dot(inv[...], prod_hi[:, c])
        y = y[:rows] + y[rows:] + dot(inv[:rows], prod_lo[:, c])
        long[t0] = y[:, :LANES]
        long[t0 + 1] = y[:, LANES:]

    @pl.when(me > 0)
    def _():
        _first, second = halo_copies()
        second.wait_recv()
        tail = halo_q[...].astype(jnp.float32)[SUB:]
        for t in range(tiles):
            x[0, t, pl.ds(0, SUB), :] = tail[:, t * LANES : (t + 1) * LANES]

    def body_q(t, _):
        gated[t] = jnp.concatenate(short(0, t), 0)
        return 0

    lax.fori_loop(0, tiles, body_q, 0)

    def gather(i, carry):
        end_copy(i, i).wait_recv()
        return carry * (a128[...] * a128[...]) + ends[i].astype(jnp.float32)

    carry = lax.fori_loop(0, pair, gather, jnp.zeros((modes, channels), jnp.float32))
    end_f[...] = jnp.where(side == 0, carry, carry * a128[...] + mate_b[...].astype(jnp.float32))
    squares[...] = jnp.zeros_like(squares)

    def body_e(t, _):
        cols = columns(t)
        step = [jnp.broadcast_to(a1[i : i + 1, cols], (SUB, LANES)) for i in range(modes)]
        w = [tailw[i, t] * end_f[i : i + 1, cols] for i in range(modes)]
        direct = skip[:, cols]
        for b in range(blocks):
            here = pl.ds(b * SUB, SUB)
            y = rounded(long[t, here, :] + tree(w))
            g = gated[t, here, :] * (y + direct * kv[t, here, :])
            gated[t, here, :] = g
            squares[here, :] += g * g
            if b < blocks - 1:
                w = [w[i] * step[i] for i in range(modes)]
        return 0

    lax.fori_loop(0, tiles, body_e, 0)

    def halves(a, axis):
        hi = a.astype(jnp.bfloat16)
        return jnp.concatenate([hi, (a - hi.astype(jnp.float32)).astype(jnp.bfloat16)], axis)

    mine = lax.dot_general(
        jnp.ones((2 * SUB, 2 * LANES), jnp.bfloat16), halves(squares[...], 1), (((1,), (1,)), ((), ())),
        preferred_element_type=jnp.float32,
    )[:SUB]
    sums[lane_rank] = mine

    def sum_copy(d, slot):
        return pltpu.make_async_remote_copy(
            src_ref=sums.at[lane_rank], dst_ref=sums.at[slot], send_sem=sum_send.at[d],
            recv_sem=sum_recv.at[slot], device_id={"tp": lax.rem(lane_rank + d, m)},
            device_id_type=pl.DeviceIdType.MESH,
        )

    for d in range(1, m):
        sum_copy(d, lane_rank).start()
    for d in range(1, m):
        sum_copy(d, lax.rem(lane_rank + d, m)).wait_recv()
    total = sums[0]
    for d in range(1, m):
        total = total + sums[d]
    inverse = 1.0 / jnp.sqrt(total / (channels * m) + 1e-05)
    spread = lax.dot_general(
        halves(inverse, 0), jnp.full((2 * SUB, LANES), 1.0 / SUB, jnp.bfloat16), (((0,), (0,)), ((), ())),
        preferred_element_type=jnp.float32,
    )

    for t in range(tiles):
        cols = slice(t * LANES, (t + 1) * LANES)
        result = gated[t] * gain[:, cols] * spread
        for k in range(blocks):
            long[t, pl.ds(k, SUB, stride=blocks), :] = result[k * SUB : (k + 1) * SUB]
        out[:, cols] = long[t].astype(jnp.bfloat16)

    @pl.when(me < n - 1)
    def _():
        first, second = halo_copies()
        first.wait_send()
        second.wait_send()

    def finish(j, _):
        end_copy(pair, j).wait_send()
        return 0

    lax.fori_loop(pair + 1, pairs_n, finish, 0)
    mate_copy.wait_send()
    for d in range(1, m):
        sum_copy(d, lane_rank).wait_send()


def solution(mesh):
    n, m = mesh.shape["ctx"], mesh.shape["tp"]

    def shards(projected, short_taps, residues, rates, skip_gain, norm_gain):
        rows, _, channels = projected.shape
        modes = rates.shape[1]
        tiles = channels // LANES
        f32, bf16 = jnp.float32, jnp.bfloat16
        fwd, inv = (jnp.asarray(a) for a in tables(rows))
        tile3 = pltpu.VMEM((tiles, rows, LANES), f32)
        modal = pltpu.VMEM((modes, tiles, SUB, LANES), f32)
        flat = pltpu.VMEM((modes, channels), f32)
        dma = pltpu.SemaphoreType.DMA
        return pl.pallas_call(
            functools.partial(kernel, n, m, modes, short_taps.shape[1], rows, channels, rows * n),
            out_shape=jax.ShapeDtypeStruct((rows, channels), bf16),
            in_specs=[pl.BlockSpec(memory_space=pltpu.HBM)] * 8,
            out_specs=pl.BlockSpec(memory_space=pltpu.VMEM),
            scratch_shapes=[
                pltpu.VMEM((2, 16, channels), bf16),
                pltpu.VMEM(projected.shape[1:2] + (rows, channels), bf16),
                pltpu.VMEM(short_taps.shape, f32), flat, flat,
                pltpu.VMEM((1, channels), f32), pltpu.VMEM((1, channels), f32),
                pltpu.VMEM(fwd.shape, bf16), pltpu.VMEM(inv.shape, bf16),
                dma((10,)),
                flat, flat,
                pltpu.VMEM((3, tiles, rows + SUB, LANES), f32),
                tile3, modal,
                pltpu.VMEM((3 * rows, channels), bf16),
                pltpu.VMEM((2 * rows, channels), f32), pltpu.VMEM((2 * rows, channels), f32),
                pltpu.VMEM((2 * rows, channels), bf16), pltpu.VMEM((2 * rows, channels), bf16),
                modal, flat, tile3, tile3,
                pltpu.VMEM((rows, LANES), f32),
                pltpu.VMEM((16, channels), bf16),
                pltpu.VMEM((16, channels), bf16),
                pltpu.VMEM((16, channels), bf16),
                flat,
                pltpu.VMEM((modes, channels), bf16),
                pltpu.VMEM((modes, channels), bf16),
                pltpu.VMEM((modes, channels), bf16),
                pltpu.VMEM((n // 2, modes, channels), bf16),
                pltpu.VMEM((m, SUB, LANES), f32),
                dma((2,)), dma((2,)), dma((n // 2,)), dma((n // 2,)), dma((m,)), dma((m,)), dma((2,)),
            ],
            compiler_params=pltpu.CompilerParams(
                collective_id=0, has_side_effects=True, vmem_limit_bytes=32 * 1024 * 1024
            ),
        )(*(
            pltpu.with_memory_space_constraint(a, pltpu.HBM)
            for a in (
                jnp.transpose(projected, (1, 0, 2)), short_taps, residues.T, rates.T,
                skip_gain[None, :], norm_gain[None, :], fwd, inv,
            )
        ))

    return jax.shard_map(
        shards,
        mesh=mesh,
        in_specs=(
            P("ctx", None, "tp"),
            P(None, None, "tp"),
            P("tp", None),
            P("tp", None),
            P("tp"),
            P("tp"),
        ),
        out_specs=P("ctx", "tp"),
        check_vma=False,
    )
```

```python
import functools
import math

import jax
import jax.numpy as jnp
import ml_dtypes
import numpy as np
from jax import lax
from jax.experimental import pallas as pl
from jax.experimental.pallas import tpu as pltpu
from jax.sharding import PartitionSpec as P

LANES = 128
SUB = 8


def tables(rows):
    freq = (np.arange(rows) + 0.5)[:, None] * (2.0 * math.pi / (2 * rows))
    angle = freq * np.arange(rows)[None, :]
    forward = np.concatenate([np.cos(angle), -np.sin(angle)], 0)
    order = np.arange(rows).reshape(SUB, rows // SUB).T.reshape(-1)
    forward = forward[:, order]
    inverse = forward.T / rows

    def pair(a):
        hi = a.astype(ml_dtypes.bfloat16)
        lo = (a - hi.astype(np.float64)).astype(ml_dtypes.bfloat16)
        return hi, lo

    f_hi, f_lo = pair(forward)
    g_hi, g_lo = pair(inverse)
    return np.concatenate([f_hi, f_lo, f_hi], 1), np.concatenate([g_hi, g_lo], 0)


def kernel(
    n, m, modes, taps_n, rows, channels, length,
    proj_h, taps_h, res_h, rates_h, skip_h, gain_h, fwd_h, inv_h,
    out,
    rim, proj, taps, res, rates, skip, gain, fwd, inv, load_sem,
    a1, a16, x, kv, state, filt, spec_f, spec_u, prod_hi, prod_lo, tailw, a128, long, gated, squares,
    send_kv, halo_kv, halo_q, end_f, end_b, mate_b, pair_b, ends, sums,
    halo_send, halo_recv, end_send, end_recv, sum_send, sum_recv, mate_sem,
):
    me = lax.axis_index("ctx")
    lane_rank = lax.axis_index("tp")
    tiles = channels // LANES
    blocks = rows // SUB
    dot = functools.partial(jnp.dot, preferred_element_type=jnp.float32)

    pairs = [
        (proj_h.at[pl.ds(1, 2), pl.ds(rows - 16, 16)], rim),
        (rates_h, rates), (res_h, res), (taps_h, taps),
        (proj_h.at[pl.ds(1, 2)], proj.at[pl.ds(1, 2)]),
        (proj_h.at[0], proj.at[0]),
        (fwd_h, fwd), (inv_h, inv), (skip_h, skip), (gain_h, gain),
    ]
    loads = [pltpu.make_async_copy(a, b, load_sem.at[i]) for i, (a, b) in enumerate(pairs)]
    for load in loads:
        load.start()

    barrier = pltpu.get_barrier_semaphore()

    def greet(target):
        pl.semaphore_signal(barrier, inc=1, device_id={"ctx": target}, device_id_type=pl.DeviceIdType.MESH)

    pair, side = lax.div(me, 2), lax.rem(me, 2)

    @pl.when(me > 0)
    def _():
        greet(me - 1)

    greet(me + 1 - 2 * side)

    def greet_like(i, _):
        greet(2 * i + side)
        return 0

    lax.fori_loop(0, pair, greet_like, 0)
    for d in range(1, m):
        pl.semaphore_signal(
            barrier, inc=1, device_id={"tp": lax.rem(lane_rank + d, m)}, device_id_type=pl.DeviceIdType.MESH
        )

    loads[0].wait()
    rim_k = rim[0].astype(jnp.float32)[SUB:]
    rim_v = rim[1].astype(jnp.float32)[SUB:]
    send_kv[...] = jnp.concatenate([rim_k, rim_v], 0).astype(jnp.bfloat16)
    def columns(t):
        return pl.ds(pl.multiple_of(t * LANES, LANES), LANES)

    def tree(terms):
        while len(terms) > 1:
            terms = [a + b for a, b in zip(terms[::2], terms[1::2])] + terms[len(terms) // 2 * 2 :]
        return terms[0]

    def rounded(a):
        return a.astype(jnp.bfloat16).astype(jnp.float32)

    sub = lax.broadcasted_iota(jnp.int32, (SUB, LANES), 0)
    odd, second, third = (sub & 1) > 0, (sub & 2) > 0, (sub & 4) > 0
    scale = 1.0 / math.sqrt(length)
    for i in (1, 2):
        loads[i].wait()
    rate_all = rates[...]
    a1[...] = jnp.exp(-rate_all / length)
    a16[...] = jnp.exp(-(rate_all * blocks) / length)
    a128[...] = jnp.exp(-(rate_all * rows) / length)

    def body_c(t, _):
        cols = columns(t)
        step = [jnp.broadcast_to(a1[i : i + 1, cols], (SUB, LANES)) for i in range(modes)]
        w = []
        for i in range(modes):
            one = a16[i : i + 1, cols]
            two = one * one
            four = two * two
            rest = jnp.where(odd, 1.0, one) * jnp.where(second, 1.0, two) * jnp.where(third, 1.0, four)
            past = jnp.where(odd, one, 1.0) * jnp.where(second, two, 1.0) * jnp.where(third, four, 1.0)
            state[i, t] = rest
            here = (res[i : i + 1, cols] * scale) * past
            w.append(here)
            tailw[i, t] = here * a1[i : i + 1, cols]
        for b in range(0, blocks, 2):
            first = tree(w)
            w = [w[i] * step[i] for i in range(modes)]
            both = jnp.concatenate([first, tree(w)], 0)
            if b < blocks - 2:
                w = [w[i] * step[i] for i in range(modes)]
            hi = both.astype(jnp.bfloat16)
            lo = (both - hi.astype(jnp.float32)).astype(jnp.bfloat16)
            filt[pl.ds(b * SUB, 2 * SUB), cols] = hi
            filt[pl.ds(rows + b * SUB, 2 * SUB), cols] = hi
            filt[pl.ds(2 * rows + b * SUB, 2 * SUB), cols] = lo
        return 0

    lax.fori_loop(0, tiles, body_c, 0)
    pl.semaphore_wait(barrier, jnp.where(me < n - 1, 1, 0) + 1 + (n // 2 - 1 - pair) + m - 1)

    def halo_copies():
        right = lax.rem(me + 1, n)
        first = pltpu.make_async_remote_copy(
            src_ref=send_kv, dst_ref=halo_kv, send_sem=halo_send.at[0], recv_sem=halo_recv.at[0],
            device_id={"ctx": right}, device_id_type=pl.DeviceIdType.MESH,
        )
        second = pltpu.make_async_remote_copy(
            src_ref=proj_h.at[0, pl.ds(rows - 16, 16)], dst_ref=halo_q, send_sem=halo_send.at[1],
            recv_sem=halo_recv.at[1], device_id={"ctx": right}, device_id_type=pl.DeviceIdType.MESH,
        )
        return first, second

    @pl.when(me < n - 1)
    def _():
        first, second = halo_copies()
        first.start()
        second.start()

    def short(g, t):
        cols = columns(t)
        tap = [jnp.broadcast_to(taps[g, j : j + 1, cols], (SUB, LANES)) for j in range(taps_n)]
        x[g, t, pl.ds(SUB, rows), :] = proj[g, :, cols].astype(jnp.float32)
        shifted = {
            k: x[g, t, pl.ds(SUB + k, SUB, stride=blocks), :] for k in range(1 - taps_n, blocks)
        }
        return [tree([tap[j] * shifted[k - j] for j in range(taps_n)]) for k in range(blocks)]

    def body_a(t, _):
        cols = columns(t)
        u = [rounded(a * b) for a, b in zip(short(1, t), short(2, t))]
        step = [jnp.broadcast_to(a1[i : i + 1, cols], (SUB, LANES)) for i in range(modes)]
        s = [u[0]] * modes
        kv[t, pl.ds(0, SUB), :] = u[0]
        for b in range(1, blocks):
            kv[t, pl.ds(b * SUB, SUB), :] = u[b]
            s = [step[i] * s[i] + u[b] for i in range(modes)]
        for i in range(modes):
            end_f[i : i + 1, cols] = jnp.sum(s[i] * state[i, t], axis=0, keepdims=True)
        return 0

    for i in (3, 4):
        loads[i].wait()
    @pl.when(me > 0)
    def _():
        first, _second = halo_copies()
        first.wait_recv()
        tail = halo_kv[...].astype(jnp.float32)
        for t in range(tiles):
            x[1, t, pl.ds(0, SUB), :] = tail[:SUB, t * LANES : (t + 1) * LANES]
            x[2, t, pl.ds(0, SUB), :] = tail[SUB:, t * LANES : (t + 1) * LANES]

    @pl.when(me == 0)
    def _():
        for g in range(3):
            for t in range(tiles):
                x[g, t, pl.ds(0, SUB), :] = jnp.zeros((SUB, LANES), jnp.float32)

    lax.fori_loop(0, tiles, body_a, 0)
    end_b[...] = end_f[...].astype(jnp.bfloat16)

    mate = me + 1 - 2 * lax.rem(me, 2)
    pairs_n = n // 2

    mate_copy = pltpu.make_async_remote_copy(
        src_ref=end_b, dst_ref=mate_b, send_sem=mate_sem.at[0], recv_sem=mate_sem.at[1],
        device_id={"ctx": mate}, device_id_type=pl.DeviceIdType.MESH,
    )
    mate_copy.start()

    def end_copy(slot, target):
        return pltpu.make_async_remote_copy(
            src_ref=pair_b, dst_ref=ends.at[slot], send_sem=end_send.at[target], recv_sem=end_recv.at[slot],
            device_id={"ctx": 2 * target + side}, device_id_type=pl.DeviceIdType.MESH,
        )

    def send_end(j, _):
        end_copy(pair, j).start()
        return 0

    for i in range(5, len(loads)):
        loads[i].wait()

    width = 2 * LANES
    groups = [slice(c, c + width) for c in range(0, channels, width)]
    for c in groups:
        t0 = c.start // LANES
        u = jnp.concatenate([kv[t0], kv[t0 + 1]], 1).astype(jnp.bfloat16)
        spec_f[:, c] = dot(fwd[...], filt[:, c])
        spec_u[:, c] = dot(fwd[:, : 2 * rows], jnp.concatenate([u, u], 0))
    mate_copy.wait_recv()
    other = mate_b[...].astype(jnp.float32)
    early = jnp.where(side == 0, end_f[...], other)
    late = jnp.where(side == 0, other, end_f[...])
    pair_b[...] = (early * a128[...] + late).astype(jnp.bfloat16)
    lax.fori_loop(pair + 1, pairs_n, send_end, 0)

    for c in groups:
        ur, ui, fr, fi = spec_u[:rows, c], spec_u[rows:, c], spec_f[:rows, c], spec_f[rows:, c]
        for at, part in ((0, ur * fr - ui * fi), (rows, ur * fi + ui * fr)):
            hi = part.astype(jnp.bfloat16)
            prod_hi[at : at + rows, c] = hi
            prod_lo[at : at + rows, c] = (part - hi.astype(jnp.float32)).astype(jnp.bfloat16)
    for c in groups:
        t0 = c.start // LANES
        y = dot(inv[...], prod_hi[:, c])
        y = y[:rows] + y[rows:] + dot(inv[:rows], prod_lo[:, c])
        long[t0] = y[:, :LANES]
        long[t0 + 1] = y[:, LANES:]

    @pl.when(me > 0)
    def _():
        _first, second = halo_copies()
        second.wait_recv()
        tail = halo_q[...].astype(jnp.float32)[SUB:]
        for t in range(tiles):
            x[0, t, pl.ds(0, SUB), :] = tail[:, t * LANES : (t + 1) * LANES]

    def body_q(t, _):
        gated[t] = jnp.concatenate(short(0, t), 0)
        return 0

    lax.fori_loop(0, tiles, body_q, 0)

    def gather(i, carry):
        end_copy(i, i).wait_recv()
        return carry * (a128[...] * a128[...]) + ends[i].astype(jnp.float32)

    carry = lax.fori_loop(0, pair, gather, jnp.zeros((modes, channels), jnp.float32))
    end_f[...] = jnp.where(side == 0, carry, carry * a128[...] + mate_b[...].astype(jnp.float32))
    squares[...] = jnp.zeros_like(squares)

    def body_e(t, _):
        cols = columns(t)
        step = [jnp.broadcast_to(a1[i : i + 1, cols], (SUB, LANES)) for i in range(modes)]
        w = [tailw[i, t] * end_f[i : i + 1, cols] for i in range(modes)]
        direct = skip[:, cols]
        for b in range(blocks):
            here = pl.ds(b * SUB, SUB)
            y = rounded(long[t, here, :] + tree(w))
            g = gated[t, here, :] * (y + direct * kv[t, here, :])
            gated[t, here, :] = g
            squares[here, :] += g * g
            if b < blocks - 1:
                w = [w[i] * step[i] for i in range(modes)]
        return 0

    lax.fori_loop(0, tiles, body_e, 0)

    def halves(a, axis):
        hi = a.astype(jnp.bfloat16)
        return jnp.concatenate([hi, (a - hi.astype(jnp.float32)).astype(jnp.bfloat16)], axis)

    mine = lax.dot_general(
        jnp.ones((2 * SUB, 2 * LANES), jnp.bfloat16), halves(squares[...], 1), (((1,), (1,)), ((), ())),
        preferred_element_type=jnp.float32,
    )[:SUB]
    sums[lane_rank] = mine

    def sum_copy(d, slot):
        return pltpu.make_async_remote_copy(
            src_ref=sums.at[lane_rank], dst_ref=sums.at[slot], send_sem=sum_send.at[d],
            recv_sem=sum_recv.at[slot], device_id={"tp": lax.rem(lane_rank + d, m)},
            device_id_type=pl.DeviceIdType.MESH,
        )

    for d in range(1, m):
        sum_copy(d, lane_rank).start()
    for d in range(1, m):
        sum_copy(d, lax.rem(lane_rank + d, m)).wait_recv()
    total = sums[0]
    for d in range(1, m):
        total = total + sums[d]
    inverse = 1.0 / jnp.sqrt(total / (channels * m) + 1e-05)
    spread = lax.dot_general(
        halves(inverse, 0), jnp.full((2 * SUB, LANES), 1.0 / SUB, jnp.bfloat16), (((0,), (0,)), ((), ())),
        preferred_element_type=jnp.float32,
    )

    for t in range(tiles):
        cols = slice(t * LANES, (t + 1) * LANES)
        result = gated[t] * gain[:, cols] * spread
        for k in range(blocks):
            long[t, pl.ds(k, SUB, stride=blocks), :] = result[k * SUB : (k + 1) * SUB]
        out[:, cols] = long[t].astype(jnp.bfloat16)

    @pl.when(me < n - 1)
    def _():
        first, second = halo_copies()
        first.wait_send()
        second.wait_send()

    def finish(j, _):
        end_copy(pair, j).wait_send()
        return 0

    lax.fori_loop(pair + 1, pairs_n, finish, 0)
    mate_copy.wait_send()
    for d in range(1, m):
        sum_copy(d, lane_rank).wait_send()


def solution(mesh):
    n, m = mesh.shape["ctx"], mesh.shape["tp"]

    def shards(projected, short_taps, residues, rates, skip_gain, norm_gain):
        rows, _, channels = projected.shape
        modes = rates.shape[1]
        tiles = channels // LANES
        f32, bf16 = jnp.float32, jnp.bfloat16
        fwd, inv = (jnp.asarray(a) for a in tables(rows))
        tile3 = pltpu.VMEM((tiles, rows, LANES), f32)
        modal = pltpu.VMEM((modes, tiles, SUB, LANES), f32)
        flat = pltpu.VMEM((modes, channels), f32)
        dma = pltpu.SemaphoreType.DMA
        return pl.pallas_call(
            functools.partial(kernel, n, m, modes, short_taps.shape[1], rows, channels, rows * n),
            out_shape=jax.ShapeDtypeStruct((rows, channels), bf16),
            in_specs=[pl.BlockSpec(memory_space=pltpu.HBM)] * 8,
            out_specs=pl.BlockSpec(memory_space=pltpu.VMEM),
            scratch_shapes=[
                pltpu.VMEM((2, 16, channels), bf16),
                pltpu.VMEM(projected.shape[1:2] + (rows, channels), bf16),
                pltpu.VMEM(short_taps.shape, f32), flat, flat,
                pltpu.VMEM((1, channels), f32), pltpu.VMEM((1, channels), f32),
                pltpu.VMEM(fwd.shape, bf16), pltpu.VMEM(inv.shape, bf16),
                dma((10,)),
                flat, flat,
                pltpu.VMEM((3, tiles, rows + SUB, LANES), f32),
                tile3, modal,
                pltpu.VMEM((3 * rows, channels), bf16),
                pltpu.VMEM((2 * rows, channels), f32), pltpu.VMEM((2 * rows, channels), f32),
                pltpu.VMEM((2 * rows, channels), bf16), pltpu.VMEM((2 * rows, channels), bf16),
                modal, flat, tile3, tile3,
                pltpu.VMEM((rows, LANES), f32),
                pltpu.VMEM((16, channels), bf16),
                pltpu.VMEM((16, channels), bf16),
                pltpu.VMEM((16, channels), bf16),
                flat,
                pltpu.VMEM((modes, channels), bf16),
                pltpu.VMEM((modes, channels), bf16),
                pltpu.VMEM((modes, channels), bf16),
                pltpu.VMEM((n // 2, modes, channels), bf16),
                pltpu.VMEM((m, SUB, LANES), f32),
                dma((2,)), dma((2,)), dma((n // 2,)), dma((n // 2,)), dma((m,)), dma((m,)), dma((2,)),
            ],
            compiler_params=pltpu.CompilerParams(
                collective_id=0, has_side_effects=True, vmem_limit_bytes=32 * 1024 * 1024
            ),
        )(*(
            pltpu.with_memory_space_constraint(a, pltpu.HBM)
            for a in (
                jnp.transpose(projected, (1, 0, 2)), short_taps, residues.T, rates.T,
                skip_gain[None, :], norm_gain[None, :], fwd, inv,
            )
        ))

    return jax.shard_map(
        shards,
        mesh=mesh,
        in_specs=(
            P("ctx", None, "tp"),
            P(None, None, "tp"),
            P("tp", None),
            P("tp", None),
            P("tp"),
            P("tp"),
        ),
        out_specs=P("ctx", "tp"),
        check_vma=False,
    )
```

```python
import functools
import math

import jax
import jax.numpy as jnp
import ml_dtypes
import numpy as np
from jax import lax
from jax.experimental import pallas as pl
from jax.experimental.pallas import tpu as pltpu
from jax.sharding import PartitionSpec as P

LANES = 128
SUB = 8


def tables(rows):
    freq = (np.arange(rows) + 0.5)[:, None] * (2.0 * math.pi / (2 * rows))
    angle = freq * np.arange(rows)[None, :]
    forward = np.concatenate([np.cos(angle), -np.sin(angle)], 0)
    inverse = forward.T / rows

    def pair(a):
        hi = a.astype(ml_dtypes.bfloat16)
        lo = (a - hi.astype(np.float64)).astype(ml_dtypes.bfloat16)
        return hi, lo

    f_hi, f_lo = pair(forward)
    g_hi, g_lo = pair(inverse)
    return np.concatenate([f_hi, f_lo, f_hi], 1), np.concatenate([g_hi, g_lo], 0)


def kernel(
    n, m, modes, taps_n, rows, channels, length,
    proj_h, taps_h, res_h, rates_h, skip_h, gain_h, fwd_h, inv_h,
    out,
    rim, proj, taps, res, rates, skip, gain, fwd, inv, load_sem,
    a1, a120, x, kv, state, state0, filt, spec_f, spec_u, prod_hi, prod_lo, tailw, a8, a128, long, gated, squares,
    send_kv, halo_kv, halo_q, end_f, end_b, mate_b, pair_b, ends, sums,
    halo_send, halo_recv, end_send, end_recv, sum_send, sum_recv, mate_sem,
):
    me = lax.axis_index("ctx")
    lane_rank = lax.axis_index("tp")
    tiles = channels // LANES
    blocks = rows // SUB
    dot = functools.partial(jnp.dot, preferred_element_type=jnp.float32)

    pairs = [
        (proj_h.at[pl.ds(1, 2), pl.ds(rows - 16, 16)], rim),
        (rates_h, rates), (res_h, res), (taps_h, taps),
        (proj_h.at[pl.ds(1, 2)], proj.at[pl.ds(1, 2)]),
        (proj_h.at[0], proj.at[0]),
        (fwd_h, fwd), (inv_h, inv), (skip_h, skip), (gain_h, gain),
    ]
    loads = [pltpu.make_async_copy(a, b, load_sem.at[i]) for i, (a, b) in enumerate(pairs)]
    for load in loads:
        load.start()

    barrier = pltpu.get_barrier_semaphore()

    def greet(target):
        pl.semaphore_signal(barrier, inc=1, device_id={"ctx": target}, device_id_type=pl.DeviceIdType.MESH)

    pair, side = lax.div(me, 2), lax.rem(me, 2)

    @pl.when(me > 0)
    def _():
        greet(me - 1)

    greet(me + 1 - 2 * side)

    def greet_like(i, _):
        greet(2 * i + side)
        return 0

    lax.fori_loop(0, pair, greet_like, 0)
    for d in range(1, m):
        pl.semaphore_signal(
            barrier, inc=1, device_id={"tp": lax.rem(lane_rank + d, m)}, device_id_type=pl.DeviceIdType.MESH
        )

    loads[0].wait()
    rim_k = rim[0].astype(jnp.float32)[SUB:]
    rim_v = rim[1].astype(jnp.float32)[SUB:]
    send_kv[...] = jnp.concatenate([rim_k, rim_v], 0).astype(jnp.bfloat16)
    def columns(t):
        return pl.ds(pl.multiple_of(t * LANES, LANES), LANES)

    def tree(terms):
        while len(terms) > 1:
            terms = [a + b for a, b in zip(terms[::2], terms[1::2])] + terms[len(terms) // 2 * 2 :]
        return terms[0]

    def rounded(a):
        return a.astype(jnp.bfloat16).astype(jnp.float32)

    sub = lax.broadcasted_iota(jnp.int32, (SUB, LANES), 0).astype(jnp.float32)
    scale = 1.0 / math.sqrt(length)
    for i in (1, 2):
        loads[i].wait()
    rate_all = rates[...]
    a1[...] = jnp.exp(-rate_all / length)
    a8[...] = jnp.exp(-(rate_all * SUB) / length)
    a120[...] = jnp.exp(-(rate_all * (rows - SUB)) / length)
    a128[...] = jnp.exp(-(rate_all * rows) / length)

    def body_c(t, _):
        cols = columns(t)
        step = [jnp.broadcast_to(a8[i : i + 1, cols], (SUB, LANES)) for i in range(modes)]
        w = []
        for i in range(modes):
            r = rates[i : i + 1, cols]
            rest = jnp.exp(-(r * (SUB - 1 - sub)) / length)
            state[i, t] = rest
            state0[i, t] = rest * a120[i : i + 1, cols]
            here = (res[i : i + 1, cols] * scale) * jnp.exp(-(r * sub) / length)
            w.append(here)
            tailw[i, t] = here * a1[i : i + 1, cols]
        for b in range(0, blocks, 2):
            first = tree(w)
            w = [w[i] * step[i] for i in range(modes)]
            both = jnp.concatenate([first, tree(w)], 0)
            if b < blocks - 2:
                w = [w[i] * step[i] for i in range(modes)]
            hi = both.astype(jnp.bfloat16)
            lo = (both - hi.astype(jnp.float32)).astype(jnp.bfloat16)
            filt[pl.ds(b * SUB, 2 * SUB), cols] = hi
            filt[pl.ds(rows + b * SUB, 2 * SUB), cols] = hi
            filt[pl.ds(2 * rows + b * SUB, 2 * SUB), cols] = lo
        return 0

    lax.fori_loop(0, tiles, body_c, 0)
    pl.semaphore_wait(barrier, jnp.where(me < n - 1, 1, 0) + 1 + (n // 2 - 1 - pair) + m - 1)

    def halo_copies():
        right = lax.rem(me + 1, n)
        first = pltpu.make_async_remote_copy(
            src_ref=send_kv, dst_ref=halo_kv, send_sem=halo_send.at[0], recv_sem=halo_recv.at[0],
            device_id={"ctx": right}, device_id_type=pl.DeviceIdType.MESH,
        )
        second = pltpu.make_async_remote_copy(
            src_ref=proj_h.at[0, pl.ds(rows - 16, 16)], dst_ref=halo_q, send_sem=halo_send.at[1],
            recv_sem=halo_recv.at[1], device_id={"ctx": right}, device_id_type=pl.DeviceIdType.MESH,
        )
        return first, second

    @pl.when(me < n - 1)
    def _():
        first, second = halo_copies()
        first.start()
        second.start()

    def short(g, t, start, count):
        cols = slice(t * LANES, (t + 1) * LANES) if isinstance(t, int) else columns(t)
        total = None
        for j in range(taps_n):
            term = taps[g, j : j + 1, cols] * x[g, t, pl.ds(SUB + start - j, count), :]
            total = term if total is None else total + term
        return total

    def body_a(t, _):
        cols = columns(t)
        for g in (1, 2):
            x[g, t, pl.ds(SUB, rows), :] = proj[g, :, cols].astype(jnp.float32)
        kv[t, pl.ds(SUB, rows - SUB), :] = rounded(
            short(1, t, SUB, rows - SUB) * short(2, t, SUB, rows - SUB)
        )
        step = [jnp.broadcast_to(a8[i : i + 1, cols], (SUB, LANES)) for i in range(modes)]
        s = [kv[t, pl.ds(SUB, SUB), :]] * modes
        for b in range(2, blocks):
            u = kv[t, pl.ds(b * SUB, SUB), :]
            s = [step[i] * s[i] + u for i in range(modes)]
        for i in range(modes):
            state[i, t] = s[i] * state[i, t]
        return 0

    for i in (3, 4):
        loads[i].wait()
    lax.fori_loop(0, tiles, body_a, 0)

    @pl.when(me > 0)
    def _():
        first, _second = halo_copies()
        first.wait_recv()
        tail = halo_kv[...].astype(jnp.float32)
        for t in range(tiles):
            x[1, t, pl.ds(0, SUB), :] = tail[:SUB, t * LANES : (t + 1) * LANES]
            x[2, t, pl.ds(0, SUB), :] = tail[SUB:, t * LANES : (t + 1) * LANES]

    @pl.when(me == 0)
    def _():
        for g in range(3):
            for t in range(tiles):
                x[g, t, pl.ds(0, SUB), :] = jnp.zeros((SUB, LANES), jnp.float32)

    for t in range(tiles):
        cols = slice(t * LANES, (t + 1) * LANES)
        u = rounded(short(1, t, 0, SUB) * short(2, t, 0, SUB))
        kv[t, pl.ds(0, SUB), :] = u
        for i in range(modes):
            end_f[i : i + 1, cols] = jnp.sum(state[i, t] + state0[i, t] * u, axis=0, keepdims=True)
    end_b[...] = end_f[...].astype(jnp.bfloat16)

    mate = me + 1 - 2 * lax.rem(me, 2)
    pairs_n = n // 2

    mate_copy = pltpu.make_async_remote_copy(
        src_ref=end_b, dst_ref=mate_b, send_sem=mate_sem.at[0], recv_sem=mate_sem.at[1],
        device_id={"ctx": mate}, device_id_type=pl.DeviceIdType.MESH,
    )
    mate_copy.start()

    def end_copy(slot, target):
        return pltpu.make_async_remote_copy(
            src_ref=pair_b, dst_ref=ends.at[slot], send_sem=end_send.at[target], recv_sem=end_recv.at[slot],
            device_id={"ctx": 2 * target + side}, device_id_type=pl.DeviceIdType.MESH,
        )

    def send_end(j, _):
        end_copy(pair, j).start()
        return 0

    for i in range(5, len(loads)):
        loads[i].wait()

    width = 2 * LANES
    groups = [slice(c, c + width) for c in range(0, channels, width)]
    for c in groups:
        t0 = c.start // LANES
        u = jnp.concatenate([kv[t0], kv[t0 + 1]], 1).astype(jnp.bfloat16)
        spec_f[:, c] = dot(fwd[...], filt[:, c])
        spec_u[:, c] = dot(fwd[:, : 2 * rows], jnp.concatenate([u, u], 0))
    mate_copy.wait_recv()
    other = mate_b[...].astype(jnp.float32)
    early = jnp.where(side == 0, end_f[...], other)
    late = jnp.where(side == 0, other, end_f[...])
    pair_b[...] = (early * a128[...] + late).astype(jnp.bfloat16)
    lax.fori_loop(pair + 1, pairs_n, send_end, 0)

    for c in groups:
        ur, ui, fr, fi = spec_u[:rows, c], spec_u[rows:, c], spec_f[:rows, c], spec_f[rows:, c]
        for at, part in ((0, ur * fr - ui * fi), (rows, ur * fi + ui * fr)):
            hi = part.astype(jnp.bfloat16)
            prod_hi[at : at + rows, c] = hi
            prod_lo[at : at + rows, c] = (part - hi.astype(jnp.float32)).astype(jnp.bfloat16)
    for c in groups:
        t0 = c.start // LANES
        y = dot(inv[...], prod_hi[:, c])
        y = y[:rows] + y[rows:] + dot(inv[:rows], prod_lo[:, c])
        long[t0] = y[:, :LANES]
        long[t0 + 1] = y[:, LANES:]

    @pl.when(me > 0)
    def _():
        _first, second = halo_copies()
        second.wait_recv()
        tail = halo_q[...].astype(jnp.float32)[SUB:]
        for t in range(tiles):
            x[0, t, pl.ds(0, SUB), :] = tail[:, t * LANES : (t + 1) * LANES]

    def body_q(t, _):
        x[0, t, pl.ds(SUB, rows), :] = proj[0, :, columns(t)].astype(jnp.float32)
        gated[t] = short(0, t, 0, rows)
        return 0

    lax.fori_loop(0, tiles, body_q, 0, unroll=2)

    def gather(i, carry):
        end_copy(i, i).wait_recv()
        return carry * (a128[...] * a128[...]) + ends[i].astype(jnp.float32)

    carry = lax.fori_loop(0, pair, gather, jnp.zeros((modes, channels), jnp.float32))
    end_f[...] = jnp.where(side == 0, carry, carry * a128[...] + mate_b[...].astype(jnp.float32))
    squares[...] = jnp.zeros_like(squares)

    def body_e(t, _):
        cols = columns(t)
        step = [jnp.broadcast_to(a8[i : i + 1, cols], (SUB, LANES)) for i in range(modes)]
        w = [tailw[i, t] * end_f[i : i + 1, cols] for i in range(modes)]
        direct = skip[:, cols]
        for b in range(blocks):
            here = pl.ds(b * SUB, SUB)
            y = rounded(long[t, here, :] + tree(w))
            g = gated[t, here, :] * (y + direct * kv[t, here, :])
            gated[t, here, :] = g
            squares[here, :] += g * g
            if b < blocks - 1:
                w = [w[i] * step[i] for i in range(modes)]
        return 0

    lax.fori_loop(0, tiles, body_e, 0, unroll=2)

    def halves(a, axis):
        hi = a.astype(jnp.bfloat16)
        return jnp.concatenate([hi, (a - hi.astype(jnp.float32)).astype(jnp.bfloat16)], axis)

    mine = lax.dot_general(
        jnp.ones((2 * SUB, 2 * LANES), jnp.bfloat16), halves(squares[...], 1), (((1,), (1,)), ((), ())),
        preferred_element_type=jnp.float32,
    )[:SUB]
    sums[lane_rank] = mine

    def sum_copy(d, slot):
        return pltpu.make_async_remote_copy(
            src_ref=sums.at[lane_rank], dst_ref=sums.at[slot], send_sem=sum_send.at[d],
            recv_sem=sum_recv.at[slot], device_id={"tp": lax.rem(lane_rank + d, m)},
            device_id_type=pl.DeviceIdType.MESH,
        )

    for d in range(1, m):
        sum_copy(d, lane_rank).start()
    for d in range(1, m):
        sum_copy(d, lax.rem(lane_rank + d, m)).wait_recv()
    total = sums[0]
    for d in range(1, m):
        total = total + sums[d]
    inverse = 1.0 / jnp.sqrt(total / (channels * m) + 1e-05)
    spread = lax.dot_general(
        halves(inverse, 0), jnp.full((2 * SUB, LANES), 1.0 / SUB, jnp.bfloat16), (((0,), (0,)), ((), ())),
        preferred_element_type=jnp.float32,
    )

    for t in range(tiles):
        cols = slice(t * LANES, (t + 1) * LANES)
        out[:, cols] = (gated[t] * gain[:, cols] * spread).astype(jnp.bfloat16)

    @pl.when(me < n - 1)
    def _():
        first, second = halo_copies()
        first.wait_send()
        second.wait_send()

    def finish(j, _):
        end_copy(pair, j).wait_send()
        return 0

    lax.fori_loop(pair + 1, pairs_n, finish, 0)
    mate_copy.wait_send()
    for d in range(1, m):
        sum_copy(d, lane_rank).wait_send()


def solution(mesh):
    n, m = mesh.shape["ctx"], mesh.shape["tp"]

    def shards(projected, short_taps, residues, rates, skip_gain, norm_gain):
        rows, _, channels = projected.shape
        modes = rates.shape[1]
        tiles = channels // LANES
        f32, bf16 = jnp.float32, jnp.bfloat16
        fwd, inv = (jnp.asarray(a) for a in tables(rows))
        tile3 = pltpu.VMEM((tiles, rows, LANES), f32)
        modal = pltpu.VMEM((modes, tiles, SUB, LANES), f32)
        flat = pltpu.VMEM((modes, channels), f32)
        dma = pltpu.SemaphoreType.DMA
        return pl.pallas_call(
            functools.partial(kernel, n, m, modes, short_taps.shape[1], rows, channels, rows * n),
            out_shape=jax.ShapeDtypeStruct((rows, channels), bf16),
            in_specs=[pl.BlockSpec(memory_space=pltpu.HBM)] * 8,
            out_specs=pl.BlockSpec(memory_space=pltpu.VMEM),
            scratch_shapes=[
                pltpu.VMEM((2, 16, channels), bf16),
                pltpu.VMEM(projected.shape[1:2] + (rows, channels), bf16),
                pltpu.VMEM(short_taps.shape, f32), flat, flat,
                pltpu.VMEM((1, channels), f32), pltpu.VMEM((1, channels), f32),
                pltpu.VMEM(fwd.shape, bf16), pltpu.VMEM(inv.shape, bf16),
                dma((10,)),
                flat, flat,
                pltpu.VMEM((3, tiles, rows + SUB, LANES), f32),
                tile3, modal, modal,
                pltpu.VMEM((3 * rows, channels), bf16),
                pltpu.VMEM((2 * rows, channels), f32), pltpu.VMEM((2 * rows, channels), f32),
                pltpu.VMEM((2 * rows, channels), bf16), pltpu.VMEM((2 * rows, channels), bf16),
                modal, flat, flat, tile3, tile3,
                pltpu.VMEM((rows, LANES), f32),
                pltpu.VMEM((16, channels), bf16),
                pltpu.VMEM((16, channels), bf16),
                pltpu.VMEM((16, channels), bf16),
                flat,
                pltpu.VMEM((modes, channels), bf16),
                pltpu.VMEM((modes, channels), bf16),
                pltpu.VMEM((modes, channels), bf16),
                pltpu.VMEM((n // 2, modes, channels), bf16),
                pltpu.VMEM((m, SUB, LANES), f32),
                dma((2,)), dma((2,)), dma((n // 2,)), dma((n // 2,)), dma((m,)), dma((m,)), dma((2,)),
            ],
            compiler_params=pltpu.CompilerParams(
                collective_id=0, has_side_effects=True, vmem_limit_bytes=32 * 1024 * 1024
            ),
        )(*(
            pltpu.with_memory_space_constraint(a, pltpu.HBM)
            for a in (
                jnp.transpose(projected, (1, 0, 2)), short_taps, residues.T, rates.T,
                skip_gain[None, :], norm_gain[None, :], fwd, inv,
            )
        ))

    return jax.shard_map(
        shards,
        mesh=mesh,
        in_specs=(
            P("ctx", None, "tp"),
            P(None, None, "tp"),
            P("tp", None),
            P("tp", None),
            P("tp"),
            P("tp"),
        ),
        out_specs=P("ctx", "tp"),
        check_vma=False,
    )
```
